256 devices in a mesh: blk: 64 (over x, z, y_hi), rep: 4 (over y_lo, core).
Axes of the slice: x: 4, y: 4 (y_hi: 2, y_lo: 2; y = y_hi * 2 + y_lo), z: 8, core: 2. Of those that a mesh axis runs over, the one named last changes fastest.
Arguments:
- activated_neurons: bfloat16 [8192, 4304], P('blk', 'rep'), may hold values from -6 to 6
- skip_stream_input: bfloat16 [8192, 1152], P('blk'), may hold values from -6 to 6
- downward_projection_weights: bfloat16 [2, 4304, 1152], P(None, 'rep'), may hold values from -0.09375 to 0.09375
- description_cluster_id: int32 [8192], P('blk'), may hold values from 0 to 2047, as said below
- score_warmth_param: float32 [1], replicated, may hold values from 5 to 20
- score_shift_term: float32 [1], replicated, may hold values from -4 to -1
Outputs:
- hidden_grad: bfloat16 [8192, 4304], P('blk', 'rep')
- weight_grad: float32 [2, 4304, 1152], P(None, 'rep', 'blk')
- loss: float32 [1], replicated
The draws below stay inside these ranges and needn't reach their ends.
Inputs may be any that keep to these rules, and one draw needn't show every extreme that they name: `description_cluster_id`: among the first 6144 rows every caption id appears exactly 3 times; among the last 2048 rows every caption id appears exactly once.
All inputs are finite; a program needn't handle non-finite values.
Results may differ from the reference program's by a relative error of at most 0.024.
Values may be sent and summed in bfloat16 or wider, within the bound.
A program may use at most 128 MiB of HBM per device.

```python
import math
import jax
import jax.numpy as jnp
from jax import lax

D = 1152
FF = 4304
NTOT = 8192
NIMG = 6144
NTXT = 2048


def draw_description_cluster_id(key, part):
    key = jax.random.fold_in(key, 7)
    image_key, text_key = jax.random.split(key)
    image_ids = jax.random.permutation(image_key, NIMG) // 3
    text_ids = jax.random.permutation(text_key, NTXT)
    return jnp.concatenate([image_ids, text_ids]).astype(jnp.int32)


def block_scale(rng, dims, cuts, smallest, top_value):
    factor_of = 1.0
    for axis_at, blocks in cuts:
        draws = jax.random.uniform(jax.random.fold_in(jax.random.fold_in(rng, 6), axis_at), (blocks,), jnp.float32, smallest / len(cuts), top_value / len(cuts))
        factor_of = factor_of * jnp.repeat(jnp.exp(draws), dims[axis_at] // blocks).reshape((-1,) + (1,) * (len(dims) - 1 - axis_at))
    return factor_of


def noise(stream_key, dims, spread, reach, shards=(), dtype=jnp.bfloat16):
    entries = spread * jax.random.normal(stream_key, dims, jnp.float32)
    if shards:
        entries = entries * block_scale(stream_key, dims, shards, -0.22, 0.18)
    return jnp.clip(entries, -reach, reach).astype(dtype)


def setup_inputs(seed: int = 0) -> dict:
    key_of = jax.random.split(jax.random.key(seed), 7)
    return {
        "activated_neurons": noise(key_of[0], (NTOT, FF), 1.0, 6.0, ((0, 64), (1, 4))),
        "skip_stream_input": noise(key_of[1], (NTOT, D), 1.0, 6.0, ((0, 64),)),
        "downward_projection_weights": noise(key_of[2], (2, FF, D), FF ** -0.5, 0.09375, ((1, 4),)),
        "description_cluster_id": draw_description_cluster_id(jax.random.fold_in(key_of[6], 71), 0),
        "score_warmth_param": jnp.clip(jnp.exp(jax.random.uniform(key_of[4], (1,), jnp.float32, math.log(5.0), math.log(20.0))), 5.0, 20.0),
        "score_shift_term": jnp.clip(jax.random.uniform(key_of[5], (1,), jnp.float32, -4.0, -1.0), -4.0, -1.0),
    }


EPS = 1e-06
OBJECTIVE_SCALE = 16.0

def reference(activated_neurons, skip_stream_input, downward_projection_weights, description_cluster_id, score_warmth_param, score_shift_term):
    branch = jnp.concatenate([jnp.dot(activated_neurons[:NIMG], downward_projection_weights[0], preferred_element_type=jnp.float32), jnp.dot(activated_neurons[NIMG:], downward_projection_weights[1], preferred_element_type=jnp.float32)], axis=0)
    pre = skip_stream_input.astype(jnp.float32) + branch
    row_norm = jnp.sqrt(lax.optimization_barrier(jnp.sum(pre * pre, axis=1, keepdims=True)) + EPS)
    unit_rows = pre / row_norm
    feature_matrix = unit_rows.astype(jnp.bfloat16)
    sharpness_factor = score_warmth_param[0]
    start_position = score_shift_term[0]
    cosine_match = jnp.dot(feature_matrix[:NIMG], feature_matrix[NIMG:].T, preferred_element_type=jnp.float32)
    couple_scores = sharpness_factor * cosine_match + start_position
    matched = description_cluster_id[:NIMG][:, None] == description_cluster_id[NIMG:][None, :]
    desired_signs = jnp.where(matched, jnp.float32(1.0), jnp.float32(-1.0))
    loss = jnp.sum(jax.nn.softplus(-desired_signs * couple_scores)) / NIMG
    couple_weight_factor = (-desired_signs * jax.nn.sigmoid(-desired_signs * couple_scores) * (OBJECTIVE_SCALE * sharpness_factor)).astype(jnp.bfloat16)
    image_grad = jnp.dot(couple_weight_factor, feature_matrix[NIMG:], preferred_element_type=jnp.float32)
    text_grad = jnp.dot(couple_weight_factor.T, feature_matrix[:NIMG], preferred_element_type=jnp.float32)
    emb_grad = jnp.concatenate([image_grad, text_grad], axis=0)
    pre_grad = ((emb_grad - unit_rows * lax.optimization_barrier(jnp.sum(unit_rows * emb_grad, axis=1, keepdims=True))) / row_norm).astype(jnp.bfloat16)
    hidden_grad = jnp.concatenate([jnp.dot(pre_grad[:NIMG], downward_projection_weights[0].T, preferred_element_type=jnp.float32), jnp.dot(pre_grad[NIMG:], downward_projection_weights[1].T, preferred_element_type=jnp.float32)], axis=0).astype(jnp.bfloat16)
    weight_grad = jnp.stack([jnp.dot(activated_neurons[:NIMG].T, pre_grad[:NIMG], preferred_element_type=jnp.float32), jnp.dot(activated_neurons[NIMG:].T, pre_grad[NIMG:], preferred_element_type=jnp.float32)], axis=0)
    return (hidden_grad, weight_grad, jnp.reshape(loss, (1,)))
```

```python
import functools

import jax
import jax.numpy as jnp
from jax import lax
from jax.experimental import pallas as pl
from jax.experimental.pallas import tpu as pltpu
from jax.sharding import PartitionSpec as P

EPS = 1e-06
OBJECTIVE_SCALE = 16.0
F32 = jnp.float32
BF16 = jnp.bfloat16
MESH = pl.DeviceIdType.MESH
NT = (((1,), (1,)), ((), ()))
TN = (((0,), (0,)), ((), ()))

NX, NZ, NY, NREP = 4, 8, 2, 4
COL = NY * NREP


def split_hi_lo(v):
    hi = v.astype(BF16)
    return hi, (v - hi.astype(F32)).astype(BF16)


def kernel(
    rows,
    width,
    ffq,
    n_img,
    at_ref,
    skip_ref,
    ids_ref,
    warm_ref,
    shift_ref,
    w_hbm,
    hid_ref,
    wg_ref,
    loss_ref,
    w_ref,
    perm_ref,
    aall,
    part,
    rsbuf,
    emb,
    txt,
    gi,
    gt,
    gir,
    gtr,
    tsum,
    tfin,
    hotb,
    gall,
    eacc,
    gts,
    gtz,
    pacc,
    pieces,
    fin,
    unit_ref,
    norm_ref,
    w_sem,
    rs_s,
    rs_r,
    img_s,
    img_r,
    tx_s,
    txt_s,
    txt_r,
    gi_s,
    gi_r,
    gt_s,
    gt_r,
    tf_s,
    tf_r,
    ga_s,
    ga_r,
    gz_s,
    gz_r,
    pc_s,
    pc_r,
    ar_s,
    al_s,
    a_r,
):
    own = rows // NREP
    d18 = width // (NX * NZ * NY)
    slab = width // NZ
    blk = lax.axis_index("blk")
    rep = lax.axis_index("rep")
    x = blk // (NZ * NY)
    z = (blk // NY) % NZ
    yh = blk % NY
    q = yh * NREP + rep
    is_img = x < NX - 1

    def dev(xx, zz, yy, rr):
        return ((xx * NZ + zz) * NY + yy, rr)

    def col_dev(qq):
        return dev(x, z, qq // NREP, qq % NREP)

    def rcopy(src, dst, ssem, rsem, device):
        return pltpu.make_async_remote_copy(
            src_ref=src, dst_ref=dst, send_sem=ssem, recv_sem=rsem, device_id=device, device_id_type=MESH
        )

    here = (blk, rep)

    def arrived(ref, rsem):
        rcopy(ref, ref, rsem, rsem, here).wait_recv()

    def left_us(ref, ssem):
        rcopy(ref, ref, ssem, ssem, here).wait_send()

    w_copy = pltpu.make_async_copy(w_hbm, w_ref, w_sem)
    w_copy.start()

    barrier = pltpu.get_barrier_semaphore()
    peers = [col_dev((q + k) % COL) for k in range(1, COL)]
    peers += [dev(x, (z + k) % NZ, yh, rep) for k in range(1, NZ)]
    peers += [dev((x + k) % NX, z, yy, rep) for k in range(1, NX) for yy in range(NY)]
    for peer in peers:
        pl.semaphore_signal(barrier, inc=1, device_id=peer, device_id_type=MESH)

    aall[z, pl.ds(ffq // 16 * 16, 16), :] = jnp.zeros((16, rows), BF16)
    aall[z, pl.ds(0, ffq), :] = at_ref[...]

    w_copy.wait()
    a_t = aall[z]
    partial = lax.dot_general(a_t, w_ref[...], TN, preferred_element_type=F32)
    part[...] = partial.astype(BF16).reshape(NREP, own, width)

    pl.semaphore_wait(barrier, len(peers))

    for k in range(1, NREP):
        r = (rep + k) % NREP
        rcopy(part.at[r], rsbuf.at[rep], rs_s.at[k], rs_r.at[rep], (blk, r)).start()

    z_r, z_l = (z + 1) % NZ, (z + NZ - 1) % NZ

    def a_step(s):
        right = (z + NZ - s) % NZ
        left = (z + s) % NZ
        if s > 0:
            arrived(aall.at[right], a_r.at[right])
        rcopy(aall.at[right], aall.at[right], ar_s.at[s], a_r.at[right], dev(x, z_r, yh, rep)).start()
        if s < NZ // 2 - 1:
            if s > 0:
                arrived(aall.at[left], a_r.at[left])
            rcopy(aall.at[left], aall.at[left], al_s.at[s], a_r.at[left], dev(x, z_l, yh, rep)).start()

    a_step(0)

    for zz in range(NZ):
        row = lax.broadcasted_iota(jnp.int32, (slab, width), 0)
        col = lax.broadcasted_iota(jnp.int32, (slab, width), 1)
        per_x = NY * d18
        wrap = jnp.zeros_like(row)
        for j in range(1, NX):
            wrap += (row >= j * per_x).astype(jnp.int32)
        source = row + wrap * (per_x * NZ - per_x) + per_x * zz
        perm_ref[pl.ds(zz * slab, slab), :] = jnp.where(source == col, 1.0, 0.0).astype(BF16)

    ids = ids_ref[...]
    feature = lax.broadcasted_iota(jnp.int32, (128, rows), 0)
    wanted = jnp.where(feature < 64, ids >> 6, (ids & 63) + 64)
    hot = jnp.where(feature == wanted, 1.0, 0.0).astype(F32)
    hotb[...] = hot.T.astype(BF16).reshape(NREP, own, 128)

    for k in range(1, NREP):
        r = (rep + k) % NREP
        arrived(rsbuf.at[r], rs_r.at[r])
    my_rows = pl.ds(pl.multiple_of(rep * own, own), own)
    branch = part[rep].astype(F32)
    for k in range(1, NREP):
        branch += rsbuf[(rep + k) % NREP].astype(F32)
    pre = skip_ref[my_rows, :].astype(F32) + branch
    row_norm = jnp.sqrt(jnp.sum(pre * pre, axis=1, keepdims=True) + EPS)
    unit = pre / row_norm
    unit_ref[...] = unit
    norm_ref[...] = jnp.broadcast_to(row_norm, (own, 128))
    emb[q, :, pl.ds(0, width)] = unit.astype(BF16)
    emb[q, :, pl.ds(width, 128)] = hotb[rep]

    warm = warm_ref[0]
    shift = shift_ref[0]
    loss_rows = (own, 128)

    @pl.when(jnp.logical_not(is_img))
    def _():
        for xx in range(NX - 1):
            rcopy(emb.at[q], txt.at[z], tx_s.at[xx], txt_r.at[z], dev(xx, z, yh, rep)).start()
        a_step(1)

    @pl.when(is_img)
    def _():
        for k in range(1, COL):
            qq = (q + k) % COL
            rcopy(emb.at[q], emb.at[q], img_s.at[k], img_r.at[q], col_dev(qq)).start()
        arrived(txt.at[z], txt_r.at[z])
        for k in range(1, NZ):
            zz = (z + k) % NZ
            rcopy(txt.at[z], txt.at[z], txt_s.at[k], txt_r.at[z], dev(x, zz, yh, rep)).start()
        a_step(1)
        for k in range(1, COL):
            qq = (q + k) % COL
            arrived(emb.at[qq], img_r.at[qq])
        for k in range(1, NZ):
            zz = (z + k) % NZ
            arrived(txt.at[zz], txt_r.at[zz])

        n_i, n_t = COL * own, NZ * own
        e_i = emb[...].reshape(n_i, width + 128)
        e_t = txt[...].reshape(n_t, width + 128)
        cosine = lax.dot_general(e_i[:, :width], e_t[:, :width], NT, preferred_element_type=F32)
        same = lax.dot_general(e_i[:, width:], e_t[:, width:], NT, preferred_element_type=F32)
        target = jnp.where(same > 1.5, 1.0, -1.0).astype(F32)
        margin = -target * (warm * cosine + shift)
        decay = jnp.exp(-jnp.abs(margin))
        softplus = jnp.maximum(margin, 0.0) + jnp.log1p(decay)
        sigmoid = jnp.where(margin >= 0.0, 1.0, decay) / (1.0 + decay)
        coef = (-target * sigmoid * (OBJECTIVE_SCALE * warm)).astype(BF16)
        grad_t = lax.dot_general(coef, e_i[:, :width], TN, preferred_element_type=F32)
        gt[...] = grad_t.astype(BF16).reshape(NZ, own, width)
        for k in range(1, NZ):
            zz = (z + k) % NZ
            rcopy(gt.at[zz], gtr.at[z], gt_s.at[k], gt_r.at[z], dev(x, zz, yh, rep)).start()
        grad_i = lax.dot_general(coef, e_t[:, :width], (((1,), (0,)), ((), ())), preferred_element_type=F32)
        gi[:, :, pl.ds(0, width)] = grad_i.astype(BF16).reshape(COL, own, width)
        loss_tile = jnp.sum(softplus, axis=0, keepdims=True)
        loss_tile = jnp.sum(loss_tile, axis=1, keepdims=True)
        l_hi, l_lo = split_hi_lo(jnp.broadcast_to(loss_tile, loss_rows))
        place = lax.broadcasted_iota(jnp.int32, loss_rows, 0)
        code = jnp.where(place == 0, l_hi.astype(F32), jnp.where(place == 1, l_lo.astype(F32), 0.0)).astype(BF16)
        for qq in range(COL):
            gi[qq, :, pl.ds(width, 128)] = code
        for k in range(1, COL):
            qq = (q + k) % COL
            rcopy(gi.at[qq], gir.at[q], gi_s.at[k], gi_r.at[q], col_dev(qq)).start()
        for k in range(1, NZ):
            zz = (z + k) % NZ
            arrived(gtr.at[zz], gt_r.at[zz])
        total = gt[z].astype(F32)
        for k in range(1, NZ):
            total += gtr[(z + k) % NZ].astype(F32)
        tsum[...] = total.astype(BF16)
        rcopy(tsum, tfin.at[x], tf_s, tf_r.at[x], dev(NX - 1, z, yh, rep)).start()

    a_step(2)

    @pl.when(is_img)
    def _():
        for k in range(1, COL):
            qq = (q + k) % COL
            arrived(gir.at[qq], gi_r.at[qq])
        total = gi[q].astype(F32)
        for k in range(1, COL):
            total += gir[(q + k) % COL].astype(F32)
        eacc[...] = total

    @pl.when(jnp.logical_not(is_img))
    def _():
        total = jnp.zeros((own, width), F32)
        for xx in range(NX - 1):
            arrived(tfin.at[xx], tf_r.at[xx])
            total += tfin[xx].astype(F32)
        eacc[:, pl.ds(0, width)] = total
        eacc[:, pl.ds(width, 128)] = jnp.zeros((own, 128), F32)

    emb_grad = eacc[:, pl.ds(0, width)]
    col_loss = jnp.sum(eacc[:, pl.ds(width, 128)], axis=0, keepdims=True)
    unit = unit_ref[...]
    along = jnp.sum(unit * emb_grad, axis=1, keepdims=True)
    pre_grad = ((emb_grad - unit * along) / norm_ref[:, :1]).astype(BF16)
    gall[rep] = pre_grad
    for k in range(1, NREP):
        r = (rep + k) % NREP
        rcopy(gall.at[rep], gall.at[rep], ga_s.at[k], ga_r.at[rep], (blk, r)).start()
    a_step(3)
    for k in range(1, NREP):
        r = (rep + k) % NREP
        arrived(gall.at[r], ga_r.at[r])

    g_block = gall[...].reshape(rows, width)
    g_t = lax.dot_general(perm_ref[...], g_block, NT, preferred_element_type=F32)
    gts[:, pl.ds(0, slab), :] = g_t.astype(BF16).reshape(NZ, slab, rows)
    l_hi, l_lo = split_hi_lo(col_loss)
    place = lax.broadcasted_iota(jnp.int32, (16, 128), 0)
    code = jnp.where(place == 0, l_hi.astype(F32), jnp.where(place == 1, l_lo.astype(F32), 0.0)).astype(BF16)
    for zz in range(NZ):
        gts[zz, pl.ds(slab, 16), :] = code
    for k in range(1, NZ):
        zz = (z + k) % NZ
        rcopy(gts.at[zz], gtz.at[z], gz_s.at[k], gz_r.at[z], dev(x, zz, yh, rep)).start()
    gtz[z] = gts[z]

    hid = lax.dot_general(w_ref[...], g_block, NT, preferred_element_type=F32)
    hid_ref[...] = hid[:ffq, :].astype(BF16)

    arrived(aall.at[(z + NZ // 2) % NZ], a_r.at[(z + NZ // 2) % NZ])
    arrived(aall.at[(z + NZ // 2 - 1) % NZ], a_r.at[(z + NZ // 2 - 1) % NZ])
    for k in range(1, NZ):
        zz = (z + k) % NZ
        arrived(gtz.at[zz], gz_r.at[zz])

    g_cat = jnp.concatenate([gtz[zz, :slab, :] for zz in range(NZ)], axis=1)
    a_cat = jnp.concatenate([aall[zz] for zz in range(NZ)], axis=1)
    pacc[pl.ds(0, slab), :] = lax.dot_general(g_cat, a_cat, NT, preferred_element_type=F32)
    pacc[pl.ds(slab, 16), :] = jnp.zeros((16, pacc.shape[1]), F32)
    plane = gtz[0, pl.ds(slab, 16), :].astype(F32)
    for zz in range(1, NZ):
        plane += gtz[zz, pl.ds(slab, 16), :].astype(F32)
    l_hi, l_lo = split_hi_lo(jnp.sum(plane, axis=0, keepdims=True))
    n_out = NX * NY
    for k in range(n_out):
        pieces[k] = pacc[pl.ds(k * d18, 32), :].astype(BF16)
        tail = pacc[pl.ds(k * d18 + 16, 16), pl.ds(0, 128)]
        tail = jnp.where(place == d18 - 16, l_hi.astype(F32), tail)
        tail = jnp.where(place == d18 - 15, l_lo.astype(F32), tail)
        pieces[k, pl.ds(16, 16), pl.ds(0, 128)] = tail.astype(BF16)
    mine = x * NY + yh
    for j in range(1, n_out):
        k = (mine + j) % n_out
        rcopy(pieces.at[k], fin.at[mine], pc_s.at[j], pc_r.at[mine], dev(k // NY, z, k % NY, rep)).start()
    fin[mine] = pieces[mine]
    for j in range(1, n_out):
        k = (mine + j) % n_out
        arrived(fin.at[k], pc_r.at[k])
    n_img_out = (NX - 1) * NY
    tower = [fin[0].astype(F32), fin[n_img_out].astype(F32)]
    for k in range(1, n_img_out):
        tower[0] += fin[k].astype(F32)
    for k in range(n_img_out + 1, n_out):
        tower[1] += fin[k].astype(F32)
    for t in range(2):
        for d in range(d18):
            wg_ref[d, pl.ds(t, 1), :] = tower[t][d : d + 1, :ffq]
    loss = jnp.zeros((1, 128), F32)
    for xx in range(NX - 1):
        last = fin[xx * NY, pl.ds(16, 16), pl.ds(0, 128)].astype(F32)
        loss += last[d18 - 16 : d18 - 15, :] + last[d18 - 15 : d18 - 14, :]
    loss_ref[0] = loss[0, 0] / n_img

    for k in range(1, NREP):
        left_us(part.at[0], rs_s.at[k])
        left_us(gall.at[0], ga_s.at[k])
    for s in range(NZ // 2):
        left_us(aall.at[0], ar_s.at[s])
    for s in range(NZ // 2 - 1):
        left_us(aall.at[0], al_s.at[s])
    for k in range(1, NZ):
        left_us(gts.at[0], gz_s.at[k])
    for j in range(1, n_out):
        left_us(pieces.at[0], pc_s.at[j])

    @pl.when(is_img)
    def _():
        for k in range(1, COL):
            left_us(emb.at[0], img_s.at[k])
            left_us(gi.at[0], gi_s.at[k])
        for k in range(1, NZ):
            left_us(txt.at[0], txt_s.at[k])
            left_us(gt.at[0], gt_s.at[k])
        left_us(tsum, tf_s)

    @pl.when(jnp.logical_not(is_img))
    def _():
        for xx in range(NX - 1):
            left_us(emb.at[0], tx_s.at[xx])


def local(
    activated_neurons,
    skip_stream_input,
    downward_projection_weights,
    description_cluster_id,
    score_warmth_param,
    score_shift_term,
):
    rows, ffq = activated_neurons.shape
    width = skip_stream_input.shape[1]
    n_blk = lax.axis_size("blk")
    d18 = width // n_blk
    own = rows // NREP
    slab = width // NZ
    ffp = -(-ffq // 16) * 16
    n_img = rows * n_blk * 3 // 4
    is_text = (lax.axis_index("blk") >= n_blk * 3 // 4).astype(jnp.int32)
    w_mine = lax.dynamic_index_in_dim(downward_projection_weights, is_text, 0, keepdims=False)
    w_mine = jnp.pad(w_mine, ((0, ffp - ffq), (0, 0)))
    vmem = pl.BlockSpec(memory_space=pltpu.VMEM)
    smem = pl.BlockSpec(memory_space=pltpu.SMEM)
    dma = pltpu.SemaphoreType.DMA
    hid_t, wg_t, loss = pl.pallas_call(
        functools.partial(kernel, rows, width, ffq, n_img),
        out_shape=(
            jax.ShapeDtypeStruct((ffq, rows), BF16),
            jax.ShapeDtypeStruct((d18, 2, ffq), F32),
            jax.ShapeDtypeStruct((1,), F32),
        ),
        in_specs=[vmem, vmem, vmem, smem, smem, pl.BlockSpec(memory_space=pl.ANY)],
        out_specs=(vmem, vmem, smem),
        scratch_shapes=[
            pltpu.VMEM((ffp, width), BF16),
            pltpu.VMEM((width, width), BF16),
            pltpu.VMEM((NZ, ffp, rows), BF16),
            pltpu.VMEM((NREP, own, width), BF16),
            pltpu.VMEM((NREP, own, width), BF16),
            pltpu.VMEM((COL, own, width + 128), BF16),
            pltpu.VMEM((NZ, own, width + 128), BF16),
            pltpu.VMEM((COL, own, width + 128), BF16),
            pltpu.VMEM((NZ, own, width), BF16),
            pltpu.VMEM((COL, own, width + 128), BF16),
            pltpu.VMEM((NZ, own, width), BF16),
            pltpu.VMEM((own, width), BF16),
            pltpu.VMEM((NX - 1, own, width), BF16),
            pltpu.VMEM((NREP, own, 128), BF16),
            pltpu.VMEM((NREP, own, width), BF16),
            pltpu.VMEM((own, width + 128), F32),
            pltpu.VMEM((NZ, slab + 16, rows), BF16),
            pltpu.VMEM((NZ, slab + 16, rows), BF16),
            pltpu.VMEM((slab + 16, ffp), F32),
            pltpu.VMEM((NX * NY, 32, ffp), BF16),
            pltpu.VMEM((NX * NY, 32, ffp), BF16),
            pltpu.VMEM((own, width), F32),
            pltpu.VMEM((own, 128), F32),
            dma,
            dma((NREP,)),
            dma((NREP,)),
            dma((COL,)),
            dma((COL,)),
            dma((NX,)),
            dma((NZ,)),
            dma((NZ,)),
            dma((COL,)),
            dma((COL,)),
            dma((NZ,)),
            dma((NZ,)),
            dma,
            dma((NX,)),
            dma((NREP,)),
            dma((NREP,)),
            dma((NZ,)),
            dma((NZ,)),
            dma((NX * NY,)),
            dma((NX * NY,)),
            dma((NZ // 2,)),
            dma((NZ // 2,)),
            dma((NZ,)),
        ],
        compiler_params=pltpu.CompilerParams(
            collective_id=0, has_side_effects=True, vmem_limit_bytes=48 * 1024 * 1024
        ),
        cost_estimate=pl.CostEstimate(flops=2 * 10**9, bytes_accessed=10**7, transcendentals=10**6),
    )(
        activated_neurons.T,
        skip_stream_input,
        description_cluster_id.reshape(1, rows),
        score_warmth_param,
        score_shift_term,
        w_mine,
    )
    return hid_t.T, jnp.transpose(wg_t, (1, 2, 0)), loss


def solution(mesh):
    placed = (P("blk", "rep"), P("blk", None), P(None, "rep", None), P("blk"), P(), P())
    return jax.shard_map(
        local,
        mesh=mesh,
        in_specs=placed,
        out_specs=(P("blk", "rep"), P(None, "rep", "blk"), P()),
        check_vma=False,
    )
```

```python
import functools

import jax
import jax.numpy as jnp
from jax import lax
from jax.experimental import pallas as pl
from jax.experimental.pallas import tpu as pltpu
from jax.sharding import PartitionSpec as P

EPS = 1e-06
OBJECTIVE_SCALE = 16.0
F32 = jnp.float32
BF16 = jnp.bfloat16
MESH = pl.DeviceIdType.MESH
NT = (((1,), (1,)), ((), ()))
TN = (((0,), (0,)), ((), ()))

NX, NZ, NY, NREP = 4, 8, 2, 4
COL = NY * NREP
NYC = 4


def split_hi_lo(v):
    hi = v.astype(BF16)
    return hi, (v - hi.astype(F32)).astype(BF16)


def kernel(
    rows,
    width,
    ffq,
    n_img,
    at_hbm,
    skip_hbm,
    ids_hbm,
    warm_ref,
    shift_ref,
    w_hbm,
    hid_ref,
    wg_ref,
    loss_ref,
    at_ref,
    skip_ref,
    ids_ref,
    wnat,
    w_ref,
    aint,
    perm_ref,
    aall,
    part,
    rsbuf,
    emb,
    txt,
    lbuf,
    gi,
    gir,
    gix_s,
    gix_r,
    gt,
    gtd,
    gtx,
    gtr,
    tsum,
    tfin,
    hotb,
    gall,
    eacc,
    gts,
    gtz,
    pacc,
    remf,
    pieces,
    fin,
    unit_ref,
    norm_ref,
    w_sem,
    in_sem,
    rs_s,
    rs_r,
    im_s,
    im_r,
    tx_s,
    tt_s,
    tt_r,
    l_s,
    l_r,
    gi_s,
    gi_r,
    gx_s,
    gx_r,
    gd_s,
    gd_r,
    gt_s,
    gt_r,
    tf_s,
    tf_r,
    ga_s,
    ga_r,
    gz_s,
    gz_r,
    gf_s,
    gf_r,
    pc_s,
    pc_r,
    ar_s,
    al_s,
    a_r,
):
    own = rows // NREP
    d18 = width // (NX * NZ * NY)
    slab = width // NZ
    blk = lax.axis_index("blk")
    rep = lax.axis_index("rep")
    x = blk // (NZ * NY)
    z = (blk // NY) % NZ
    yh = blk % NY
    y = yh * 2 + rep // 2
    core = rep % 2
    other = 1 - core
    par = z % 2
    sign = 1 - 2 * par
    z_pair = z + 1 - 2 * par
    is_img = x < NX - 1

    def dev(xx, zz, yy, rr):
        return ((xx * NZ + zz) * NY + yy, rr)

    def z_at(offset):
        return (z + NZ + offset) % NZ

    def at_y(xx, zz, yy, cc):
        return dev(xx, zz, yy // 2, (yy % 2) * 2 + cc)

    def rcopy(src, dst, ssem, rsem, device):
        return pltpu.make_async_remote_copy(
            src_ref=src, dst_ref=dst, send_sem=ssem, recv_sem=rsem, device_id=device, device_id_type=MESH
        )

    here = (blk, rep)

    def arrived(ref, rsem):
        rcopy(ref, ref, rsem, rsem, here).wait_recv()

    sent = {"all": [], "img": [], "txt": []}

    def send(group, src, dst, ssem, rsem, device):
        sem, k = ssem
        rcopy(src, dst, sem if k is None else sem.at[k], rsem, device).start()
        base = src.ref if hasattr(src, "ref") else src
        entry = (base, len(base.shape) - len(src.shape), sem, k)
        if all(e[2] is not sem or e[3] != k for e in sent[group]):
            sent[group].append(entry)

    def all_left(group):
        for ref, block, sem, k in sent[group]:
            ref = ref.at[(0,) * block] if block else ref
            sem = sem if k is None else sem.at[k]
            rcopy(ref, ref, sem, sem, here).wait_send()

    barrier = pltpu.get_barrier_semaphore()
    peers = [at_y(x, z, (y + k) % NYC, core) for k in range(1, NYC)]
    peers += [dev(x, z, yh, (rep // 2) * 2 + other), dev(x, z, yh, (1 - rep // 2) * 2 + other)]
    peers += [dev(x, (z + k) % NZ, yh, rep) for k in range(1, NZ)]
    peers += [dev((x + k) % NX, z, yy, rep) for k in range(1, NX) for yy in range(NY)]
    for peer in peers:
        pl.semaphore_signal(barrier, inc=1, device_id=peer, device_id_type=MESH)

    a_copy = pltpu.make_async_copy(at_hbm, at_ref, in_sem.at[0])
    a_copy.start()
    n_cut = 2
    step = ffq // n_cut
    cuts = [pl.ds(c * step, step) for c in range(n_cut)]
    w_copies = [pltpu.make_async_copy(w_hbm.at[cut], wnat.at[cut], w_sem.at[c]) for c, cut in enumerate(cuts)]
    for copy in w_copies:
        copy.start()
    skip_copy = pltpu.make_async_copy(skip_hbm, skip_ref, in_sem.at[1])
    ids_copy = pltpu.make_async_copy(ids_hbm, ids_ref, in_sem.at[2])
    skip_copy.start()
    ids_copy.start()

    aint[...] = jnp.zeros_like(aint)
    a_copy.wait()
    for t in range(2):

        @pl.when(is_img if t == 0 else jnp.logical_not(is_img))
        def _():
            aint[pl.ds(t, ffq, stride=2), :] = at_ref[...].astype(F32)

    a_int = aint[...].astype(BF16)
    aall[z, pl.ds(ffq // 16 * 16, 16), :] = jnp.zeros((16, rows), BF16)
    aall[z, pl.ds(0, ffq), :] = at_ref[...]
    partial = jnp.zeros((rows, width), F32)
    for c, copy in enumerate(w_copies):
        copy.wait()
        both = pl.ds(2 * c * step, 2 * step)
        w_ref[both, :] = wnat[cuts[c]].reshape(2 * step, width)
        partial += lax.dot_general(a_int[2 * c * step : 2 * (c + 1) * step], w_ref[both, :], TN, preferred_element_type=F32)
    part[...] = partial.astype(BF16).reshape(NREP, own, width)

    pl.semaphore_wait(barrier, len(peers))

    for k in range(1, NREP):
        r = (rep + k) % NREP
        send("all", part.at[r], rsbuf.at[rep], (rs_s, k), rs_r.at[rep], (blk, r))

    z_r, z_l = (z + 1) % NZ, (z + NZ - 1) % NZ

    def a_step(s):
        right = (z + NZ - s) % NZ
        left = (z + s) % NZ
        if s > 0:
            arrived(aall.at[right], a_r.at[right])
        send("all", aall.at[right], aall.at[right], (ar_s, s), a_r.at[right], dev(x, z_r, yh, rep))
        if s < NZ // 2 - 1:
            if s > 0:
                arrived(aall.at[left], a_r.at[left])
            send("all", aall.at[left], aall.at[left], (al_s, s), a_r.at[left], dev(x, z_l, yh, rep))

    def finish():
        all_left("all")

        @pl.when(is_img)
        def _():
            all_left("img")

        @pl.when(jnp.logical_not(is_img))
        def _():
            all_left("txt")

    a_step(0)

    part_rows = (slab + 16) // 2
    row = lax.broadcasted_iota(jnp.int32, (part_rows, width), 0) + core * part_rows
    col = lax.broadcasted_iota(jnp.int32, (part_rows, width), 1)
    per_x = NY * d18
    wrap = jnp.zeros_like(row)
    for k in range(1, NX):
        wrap += (row >= k * per_x).astype(jnp.int32)
    source = row + wrap * (per_x * NZ - per_x)
    for zz in range(NZ):
        perm_ref[pl.ds(zz * part_rows, part_rows), :] = jnp.where(source + per_x * zz == col, 1.0, 0.0).astype(BF16)

    ids_copy.wait()
    skip_copy.wait()
    ids = ids_ref[...]
    feature = lax.broadcasted_iota(jnp.int32, (128, rows), 0)
    wanted = jnp.where(feature < 64, ids >> 6, (ids & 63) + 64)
    hot = jnp.where(feature == wanted, 1.0, 0.0).astype(F32)
    hotb[...] = hot.T.astype(BF16).reshape(NREP, own, 128)

    for k in range(1, NREP):
        r = (rep + k) % NREP
        arrived(rsbuf.at[r], rs_r.at[r])
    my_rows = pl.ds(pl.multiple_of(rep * own, own), own)
    branch = part[rep].astype(F32)
    for k in range(1, NREP):
        branch += rsbuf[(rep + k) % NREP].astype(F32)
    pre = skip_ref[my_rows, :].astype(F32) + branch
    row_norm = jnp.sqrt(jnp.sum(pre * pre, axis=1, keepdims=True) + EPS)
    unit = pre / row_norm
    unit_ref[...] = unit
    mine_i = 2 * y + par
    mine_t = 4 * core
    norm_ref[...] = jnp.broadcast_to(row_norm, (own, 128))
    emb[mine_i, :, pl.ds(0, width)] = unit.astype(BF16)
    emb[mine_i, :, pl.ds(width, 128)] = hotb[rep]

    warm = warm_ref[0]
    shift = shift_ref[0]
    loss_rows = (own, 128)

    @pl.when(jnp.logical_not(is_img))
    def _():
        for xx in range(NX - 1):
            send("txt", emb.at[mine_i], txt.at[mine_t], (tx_s, xx), tt_r.at[mine_t], dev(xx, z, yh, rep))
        a_step(1)

    @pl.when(is_img)
    def _():
        send("img", emb.at[mine_i], emb.at[mine_i], (im_s, 0), im_r.at[mine_i], dev(x, z_pair, yh, rep))
        for k in range(1, NYC):
            send("img", emb.at[mine_i], emb.at[mine_i], (im_s, k), im_r.at[mine_i], at_y(x, z, (y + k) % NYC, core))
        arrived(txt.at[mine_t], tt_r.at[mine_t])
        for k in (3, 2, 1):
            zz = z_at(2 * sign if k == 2 else -k * sign)
            send("img", txt.at[mine_t], txt.at[mine_t + k], (tt_s, k), tt_r.at[mine_t + k], dev(x, zz, yh, rep))
        send("img", txt.at[mine_t], txt.at[mine_t], (tt_s, 0), tt_r.at[mine_t], at_y(x, z, y, other))
        pair_i = 2 * y + 1 - par
        arrived(emb.at[pair_i], im_r.at[pair_i])
        for k in range(1, NYC):
            send("img", emb.at[pair_i], emb.at[pair_i], (im_s, 3 + k), im_r.at[pair_i], at_y(x, z, (y + k) % NYC, core))
        a_step(1)
        for k in range(1, NZ // 2):
            slot = mine_t + k
            arrived(txt.at[slot], tt_r.at[slot])
            send("img", txt.at[slot], txt.at[slot], (tt_s, 3 + k), tt_r.at[slot], at_y(x, z, y, other))
        for k in range(1, NYC):
            for p in range(2):
                slot = 2 * ((y + k) % NYC) + p
                arrived(emb.at[slot], im_r.at[slot])
        for k in range(NZ // 2):
            slot = 4 * other + k
            arrived(txt.at[slot], tt_r.at[slot])

        n_i, n_t = COL * own, NZ * own
        e_i = emb[...].reshape(n_i, width + 128)
        e_t = txt[...].reshape(n_t, width + 128)
        cosine = lax.dot_general(e_i[:, :width], e_t[:, :width], NT, preferred_element_type=F32)
        same = lax.dot_general(e_i[:, width:], e_t[:, width:], NT, preferred_element_type=F32)
        target = jnp.where(same > 1.5, 1.0, -1.0).astype(F32)
        margin = -target * (warm * cosine + shift)
        decay = jnp.exp(-jnp.abs(margin))
        softplus = jnp.maximum(margin, 0.0) + jnp.log1p(decay)
        sigmoid = jnp.where(margin >= 0.0, 1.0, decay) / (1.0 + decay)
        coef = (-target * sigmoid * (OBJECTIVE_SCALE * warm)).astype(BF16)
        loss_tile = jnp.sum(softplus, axis=0, keepdims=True)
        loss_tile = jnp.sum(loss_tile, axis=1, keepdims=True)
        lbuf[0] = jnp.broadcast_to(loss_tile, (8, 128))
        send("img", lbuf.at[0], lbuf.at[1], (l_s, None), l_r, at_y(x, z, y, other))
        grad_t = lax.dot_general(coef, e_i[:, :width], TN, preferred_element_type=F32)
        gt[...] = grad_t.astype(BF16).reshape(2, NZ // 2, own, width)
        send("img", gt.at[other], gtd, (gd_s, None), gd_r, at_y(x, z, y, other))
        grad_i = lax.dot_general(coef, e_t[:, :width], (((1,), (0,)), ((), ())), preferred_element_type=F32)
        gi[:, :, :, pl.ds(0, width)] = grad_i.astype(BF16).reshape(NYC, 2, own, width)
        arrived(lbuf.at[1], l_r)
        l_hi, l_lo = split_hi_lo((lbuf[0] + lbuf[1])[:1, :])
        place = lax.broadcasted_iota(jnp.int32, (own, 128), 0)
        code = jnp.where(place == 0, l_hi.astype(F32), jnp.where(place == 1, l_lo.astype(F32), 0.0)).astype(BF16)
        for yy in range(NYC):
            for p in range(2):
                gi[yy, p, :, pl.ds(width, 128)] = code
        for k in range(1, NYC):
            yy = (y + k) % NYC
            send("img", gi.at[yy], gir.at[y], (gi_s, k), gi_r.at[y], at_y(x, z, yy, core))
        arrived(gtd, gd_r)
        gtx[...] = (gt[core].astype(F32) + gtd[...].astype(F32)).astype(BF16)
        for k in (3, 2, 1):
            send("img", gtx.at[k], gtr.at[k], (gt_s, k), gt_r.at[k], dev(x, z_at(-k * sign), yh, rep))
        a_step(2)
        for k in range(1, NYC):
            yy = (y + k) % NYC
            arrived(gir.at[yy], gi_r.at[yy])
        away = gi[y, 1 - par].astype(F32)
        kept = gi[y, par].astype(F32)
        for k in range(1, NYC):
            away += gir[(y + k) % NYC, 1 - par].astype(F32)
            kept += gir[(y + k) % NYC, par].astype(F32)
        gix_s[...] = away.astype(BF16)
        send("img", gix_s, gix_r, (gx_s, None), gx_r, dev(x, z_pair, yh, rep))
        for k in range(1, NZ // 2):
            arrived(gtr.at[k], gt_r.at[k])
        total = gtx[0].astype(F32)
        for k in range(1, NZ // 2):
            total += gtr[k].astype(F32)
        tsum[...] = total.astype(BF16)
        send("img", tsum, tfin.at[x], (tf_s, None), tf_r.at[x], dev(NX - 1, z, yh, rep))
        arrived(gix_r, gx_r)
        eacc[:, pl.ds(0, width)] = kept[:, :width] + gix_r[:, pl.ds(0, width)].astype(F32)
        eacc[:, pl.ds(width, 128)] = kept[:, width:]

    @pl.when(jnp.logical_not(is_img))
    def _():
        a_step(2)
        total = jnp.zeros((own, width), F32)
        for xx in range(NX - 1):
            arrived(tfin.at[xx], tf_r.at[xx])
            total += tfin[xx].astype(F32)
        eacc[:, pl.ds(0, width)] = total
        eacc[:, pl.ds(width, 128)] = jnp.zeros((own, 128), F32)

    emb_grad = eacc[:, pl.ds(0, width)]
    col_loss = jnp.sum(eacc[:, pl.ds(width, 128)], axis=0, keepdims=True)
    unit = unit_ref[...]
    along = jnp.sum(unit * emb_grad, axis=1, keepdims=True)
    pre_grad = ((emb_grad - unit * along) / norm_ref[:, :1]).astype(BF16)
    gall[rep] = pre_grad
    for k in range(1, NREP):
        r = (rep + k) % NREP
        send("all", gall.at[rep], gall.at[rep], (ga_s, k), ga_r.at[rep], (blk, r))
    a_step(3)
    for k in range(1, NREP):
        r = (rep + k) % NREP
        arrived(gall.at[r], ga_r.at[r])

    g_block = gall[...].reshape(rows, width)
    g_t = lax.dot_general(perm_ref[...], g_block, NT, preferred_element_type=F32)
    gts[...] = g_t.astype(BF16).reshape(NZ, part_rows, rows)
    l_hi, l_lo = split_hi_lo(col_loss)
    place = lax.broadcasted_iota(jnp.int32, (16, 128), 0)
    code = jnp.where(place == 0, l_hi.astype(F32), jnp.where(place == 1, l_lo.astype(F32), 0.0)).astype(BF16)

    @pl.when(core == 1)
    def _():
        for zz in range(NZ):
            gts[zz, pl.ds(part_rows - 16, 16), :] = code

    for i, k in enumerate((4, 3, 5, 2, 6, 1, 7)):
        send("all", gts.at[z_at(k)], gtz.at[z, core], (gz_s, i), gz_r.at[z], dev(x, z_at(k), yh, rep))
    gtz[z, core] = gts[z]
    send("all", gtz.at[z, core], gtz.at[z, core], (gf_s, 0), gf_r.at[z], at_y(x, z, y, other))

    aint[...] = lax.dot_general(w_ref[...], g_block, NT, preferred_element_type=F32)
    for t in range(2):

        @pl.when(is_img if t == 0 else jnp.logical_not(is_img))
        def _():
            hid_ref[...] = aint[pl.ds(t, ffq, stride=2), :].astype(BF16)

    arrived(aall.at[(z + NZ // 2) % NZ], a_r.at[(z + NZ // 2) % NZ])
    arrived(aall.at[(z + NZ // 2 - 1) % NZ], a_r.at[(z + NZ // 2 - 1) % NZ])
    for i, k in enumerate((1, 7, 2, 6, 3, 5, 4)):
        zz = z_at(k)
        arrived(gtz.at[zz, core], gz_r.at[zz])
        send("all", gtz.at[zz, core], gtz.at[zz, core], (gf_s, i + 1), gf_r.at[zz], at_y(x, z, y, other))
    for k in range(NZ):
        arrived(gtz.at[z_at(k), other], gf_r.at[z_at(k)])

    rest = slab - part_rows
    g_cat = jnp.concatenate(
        [jnp.concatenate([gtz[zz, 0], gtz[zz, 1, :rest, :]], axis=0) for zz in range(NZ)], axis=1
    )
    a_cat = jnp.concatenate([aall[zz] for zz in range(NZ)], axis=1)
    lanes = pacc.shape[1]
    pacc[:, pl.ds(lanes - 128, 128)] = jnp.zeros((slab, 128), F32)
    pacc[:, pl.ds(0, a_cat.shape[0])] = lax.dot_general(g_cat, a_cat, NT, preferred_element_type=F32)
    plane = gtz[0, 1, pl.ds(rest, 16), :].astype(F32)
    for zz in range(1, NZ):
        plane += gtz[zz, 1, pl.ds(rest, 16), :].astype(F32)
    l_hi, l_lo = split_hi_lo(jnp.sum(plane, axis=0, keepdims=True))
    extra = jnp.where(place == 1, l_hi.astype(F32), jnp.where(place == 2, l_lo.astype(F32), 0.0))
    n_out = NX * NY
    full = lanes // 128 - 1
    for k in range(n_out):
        remf[k, :, pl.ds(128, 128)] = extra
        for i in range(d18 - 16):
            row = k * d18 + 16 + i
            for c in range(full):
                remf[k, pl.ds(8 * i + c, 1), pl.ds(0, 128)] = pacc[pl.ds(row, 1), pl.ds(c * 128, 128)]
            remf[k, pl.ds(8 * i, 1), pl.ds(128, 128)] = pacc[pl.ds(row, 1), pl.ds(full * 128, 128)]
        pieces[k, :, pl.ds(0, lanes)] = pacc[pl.ds(k * d18, 16), :].astype(BF16)
        pieces[k, :, pl.ds(lanes, 256)] = remf[k].astype(BF16)
    mine = x * NY + yh
    for i, (dx, dy) in enumerate(((2, 1), (1, 1), (3, 1), (2, 0), (0, 1), (1, 0), (3, 0))):
        xx, yy = (x + dx) % NX, (yh + dy) % NY
        send("all", pieces.at[xx * NY + yy], fin.at[mine], (pc_s, i), pc_r.at[mine], dev(xx, z, yy, rep))
    fin[mine] = pieces[mine]
    for j in range(1, n_out):
        k = (mine + j) % n_out
        arrived(fin.at[k], pc_r.at[k])
    n_img_out = (NX - 1) * NY
    tower = [fin[0].astype(F32), fin[n_img_out].astype(F32)]
    for k in range(1, n_img_out):
        tower[0] += fin[k].astype(F32)
    for k in range(n_img_out + 1, n_out):
        tower[1] += fin[k].astype(F32)
    for t in range(2):
        for d in range(16):
            wg_ref[d, pl.ds(t, 1), :] = tower[t][d : d + 1, :ffq]
        for i in range(d18 - 16):
            for c in range(full):
                wg_ref[16 + i, pl.ds(t, 1), pl.ds(c * 128, 128)] = tower[t][8 * i + c : 8 * i + c + 1, lanes : lanes + 128]
            last = ffq - full * 128
            wg_ref[16 + i, pl.ds(t, 1), pl.ds(full * 128, last)] = tower[t][8 * i : 8 * i + 1, lanes + 128 : lanes + 128 + last]
    both = tower[0][1, lanes + 128] + tower[0][2, lanes + 128]
    loss_ref[0] = both / (NY * n_img)

    finish()


def local(
    activated_neurons,
    skip_stream_input,
    downward_projection_weights,
    description_cluster_id,
    score_warmth_param,
    score_shift_term,
):
    rows, ffq = activated_neurons.shape
    width = skip_stream_input.shape[1]
    n_blk = lax.axis_size("blk")
    d18 = width // n_blk
    own = rows // NREP
    slab = width // NZ
    ffp = -(-ffq // 16) * 16
    n_img = rows * n_blk * 3 // 4
    lanes = -(-ffq // 128) * 128
    vmem = pl.BlockSpec(memory_space=pltpu.VMEM)
    hbm = pl.BlockSpec(memory_space=pl.ANY)
    smem = pl.BlockSpec(memory_space=pltpu.SMEM)
    dma = pltpu.SemaphoreType.DMA
    hid_t, wg_t, loss = pl.pallas_call(
        functools.partial(kernel, rows, width, ffq, n_img),
        out_shape=(
            jax.ShapeDtypeStruct((ffq, rows), BF16),
            jax.ShapeDtypeStruct((d18, 2, ffq), F32),
            jax.ShapeDtypeStruct((1,), F32),
        ),
        in_specs=[hbm, hbm, hbm, smem, smem, hbm],
        out_specs=(vmem, vmem, smem),
        scratch_shapes=[
            pltpu.VMEM((ffq, rows), BF16),
            pltpu.VMEM((rows, width), BF16),
            pltpu.VMEM((1, rows), jnp.int32),
            pltpu.VMEM((ffq, 2, width), BF16),
            pltpu.VMEM((2 * ffq, width), BF16),
            pltpu.VMEM((2 * ffq, rows), F32),
            pltpu.VMEM((NZ * (slab + 16) // 2, width), BF16),
            pltpu.VMEM((NZ, ffp, rows), BF16),
            pltpu.VMEM((NREP, own, width), BF16),
            pltpu.VMEM((NREP, own, width), BF16),
            pltpu.VMEM((COL, own, width + 128), BF16),
            pltpu.VMEM((NZ, own, width + 128), BF16),
            pltpu.VMEM((2, 8, 128), F32),
            pltpu.VMEM((NYC, 2, own, width + 128), BF16),
            pltpu.VMEM((NYC, 2, own, width + 128), BF16),
            pltpu.VMEM((own, width + 128), BF16),
            pltpu.VMEM((own, width + 128), BF16),
            pltpu.VMEM((2, NZ // 2, own, width), BF16),
            pltpu.VMEM((NZ // 2, own, width), BF16),
            pltpu.VMEM((NZ // 2, own, width), BF16),
            pltpu.VMEM((NZ // 2, own, width), BF16),
            pltpu.VMEM((own, width), BF16),
            pltpu.VMEM((NX - 1, own, width), BF16),
            pltpu.VMEM((NREP, own, 128), BF16),
            pltpu.VMEM((NREP, own, width), BF16),
            pltpu.VMEM((own, width + 128), F32),
            pltpu.VMEM((NZ, (slab + 16) // 2, rows), BF16),
            pltpu.VMEM((NZ, 2, (slab + 16) // 2, rows), BF16),
            pltpu.VMEM((slab, lanes), F32),
            pltpu.VMEM((NX * NY, 16, 256), F32),
            pltpu.VMEM((NX * NY, 16, lanes + 256), BF16),
            pltpu.VMEM((NX * NY, 16, lanes + 256), BF16),
            pltpu.VMEM((own, width), F32),
            pltpu.VMEM((own, 128), F32),
            dma((4,)),
            dma((3,)),
            dma((NREP,)),
            dma((NREP,)),
            dma((7,)),
            dma((COL,)),
            dma((NX,)),
            dma((7,)),
            dma((NZ,)),
            dma,
            dma,
            dma((NYC,)),
            dma((NYC,)),
            dma,
            dma,
            dma,
            dma,
            dma((NZ // 2,)),
            dma((NZ // 2,)),
            dma,
            dma((NX,)),
            dma((NREP,)),
            dma((NREP,)),
            dma((NZ,)),
            dma((NZ,)),
            dma((NZ,)),
            dma((NZ,)),
            dma((NX * NY,)),
            dma((NX * NY,)),
            dma((NZ // 2,)),
            dma((NZ // 2,)),
            dma((NZ,)),
        ],
        compiler_params=pltpu.CompilerParams(
            collective_id=0, has_side_effects=True, vmem_limit_bytes=53 * 1024 * 1024
        ),
        cost_estimate=pl.CostEstimate(flops=2 * 10**9, bytes_accessed=10**7, transcendentals=10**6),
    )(
        activated_neurons.T,
        skip_stream_input,
        description_cluster_id.reshape(1, rows),
        score_warmth_param,
        score_shift_term,
        jnp.transpose(downward_projection_weights, (1, 0, 2)),
    )
    return hid_t.T, jnp.transpose(wg_t, (1, 2, 0)), loss


def solution(mesh):
    placed = (P("blk", "rep"), P("blk", None), P(None, "rep", None), P("blk"), P(), P())
    return jax.shard_map(
        local,
        mesh=mesh,
        in_specs=placed,
        out_specs=(P("blk", "rep"), P(None, "rep", "blk"), P()),
        check_vma=False,
    )
```

```python
import functools

import jax
import jax.numpy as jnp
from jax import lax
from jax.experimental import pallas as pl
from jax.experimental.pallas import tpu as pltpu
from jax.sharding import PartitionSpec as P

EPS = 1e-06
OBJECTIVE_SCALE = 16.0
F32 = jnp.float32
BF16 = jnp.bfloat16
MESH = pl.DeviceIdType.MESH
NT = (((1,), (1,)), ((), ()))
TN = (((0,), (0,)), ((), ()))

NX, NZ, NY, NREP = 4, 8, 2, 4
COL = NY * NREP
NYC = 4


def split_hi_lo(v):
    hi = v.astype(BF16)
    return hi, (v - hi.astype(F32)).astype(BF16)


def kernel(
    rows,
    width,
    ffq,
    n_img,
    at_hbm,
    skip_hbm,
    ids_hbm,
    warm_ref,
    shift_ref,
    w_hbm,
    hid_ref,
    wg_ref,
    loss_ref,
    at_ref,
    skip_ref,
    ids_ref,
    wnat,
    w_ref,
    aint,
    perm_ref,
    aall,
    part,
    rsbuf,
    emb,
    txt,
    lbuf,
    gi,
    gid,
    gaway,
    garr,
    gsum,
    gir,
    gix_s,
    gix_r,
    gtx,
    gtr,
    tsum,
    tfin,
    hotb,
    gall,
    eacc,
    gts,
    gtz,
    pacc,
    remf,
    pieces,
    fin,
    unit_ref,
    norm_ref,
    w_sem,
    in_sem,
    rs_s,
    rs_r,
    im_s,
    ic_s,
    im_r,
    tx_s,
    tt_s,
    tt_r,
    l_s,
    l_r,
    go_s,
    go_r,
    gi_s,
    gi_r,
    gx_s,
    gx_r,
    gd_s,
    gd_r,
    gt_s,
    gt_r,
    tf_s,
    tf_r,
    ga_s,
    ga_r,
    gz_s,
    gz_r,
    gf_s,
    gf_r,
    pc_s,
    pc_r,
    ar_s,
    al_s,
    a_r,
    a2_r,
):
    own = rows // NREP
    d18 = width // (NX * NZ * NY)
    slab = width // NZ
    blk = lax.axis_index("blk")
    rep = lax.axis_index("rep")
    x = blk // (NZ * NY)
    z = (blk // NY) % NZ
    yh = blk % NY
    y = yh * 2 + rep // 2
    core = rep % 2
    other = 1 - core
    par = z % 2
    sign = 1 - 2 * par
    z_pair = z + 1 - 2 * par
    is_img = x < NX - 1

    def dev(xx, zz, yy, rr):
        return ((xx * NZ + zz) * NY + yy, rr)

    def z_at(offset):
        return (z + NZ + offset) % NZ

    def at_y(xx, zz, yy, cc):
        return dev(xx, zz, yy // 2, (yy % 2) * 2 + cc)

    def rcopy(src, dst, ssem, rsem, device):
        return pltpu.make_async_remote_copy(
            src_ref=src, dst_ref=dst, send_sem=ssem, recv_sem=rsem, device_id=device, device_id_type=MESH
        )

    here = (blk, rep)

    def arrived(ref, rsem):
        rcopy(ref, ref, rsem, rsem, here).wait_recv()

    sent = {"all": [], "img": [], "txt": []}

    def send(group, src, dst, ssem, rsem, device):
        sem, k = ssem
        rcopy(src, dst, sem if k is None else sem.at[k], rsem, device).start()
        base = src.ref if hasattr(src, "ref") else src
        entry = (base, len(base.shape) - len(src.shape), sem, k)
        if all(e[2] is not sem or e[3] != k for e in sent[group]):
            sent[group].append(entry)

    def all_left(group):
        for ref, block, sem, k in sent[group]:
            ref = ref.at[(0,) * block] if block else ref
            sem = sem if k is None else sem.at[k]
            rcopy(ref, ref, sem, sem, here).wait_send()

    barrier = pltpu.get_barrier_semaphore()
    peers = [at_y(x, z, (y + k) % NYC, core) for k in range(1, NYC)]
    peers += [dev(x, z, yh, (rep // 2) * 2 + other), dev(x, z, yh, (1 - rep // 2) * 2 + other)]
    peers += [dev(x, (z + k) % NZ, yh, rep) for k in range(1, NZ)]
    peers += [dev((x + k) % NX, z, yy, rep) for k in range(1, NX) for yy in range(NY)]
    for peer in peers:
        pl.semaphore_signal(barrier, inc=1, device_id=peer, device_id_type=MESH)

    a_copy = pltpu.make_async_copy(at_hbm, at_ref, in_sem.at[0])
    a_copy.start()
    n_cut = 2
    step = ffq // n_cut
    cuts = [pl.ds(c * step, step) for c in range(n_cut)]
    w_copies = [pltpu.make_async_copy(w_hbm.at[cut], wnat.at[cut], w_sem.at[c]) for c, cut in enumerate(cuts)]
    for copy in w_copies:
        copy.start()
    skip_copy = pltpu.make_async_copy(skip_hbm, skip_ref, in_sem.at[1])
    ids_copy = pltpu.make_async_copy(ids_hbm, ids_ref, in_sem.at[2])
    skip_copy.start()
    ids_copy.start()

    aint[...] = jnp.zeros_like(aint)
    a_copy.wait()
    for t in range(2):

        @pl.when(is_img if t == 0 else jnp.logical_not(is_img))
        def _():
            aint[pl.ds(t, ffq, stride=2), :] = at_ref[...].astype(F32)

    a_int = aint[...].astype(BF16)
    a_half = aall.shape[2]
    aall[z, 1, pl.ds(a_half - 16, 16), :] = jnp.zeros((16, rows), BF16)
    aall[z, 0] = at_ref[pl.ds(0, a_half), :]
    aall[z, 1, pl.ds(0, ffq - a_half), :] = at_ref[pl.ds(a_half, ffq - a_half), :]
    partial = jnp.zeros((rows, width), F32)
    for c, copy in enumerate(w_copies):
        copy.wait()
        both = pl.ds(2 * c * step, 2 * step)
        w_ref[both, :] = wnat[cuts[c]].reshape(2 * step, width)
        partial += lax.dot_general(a_int[2 * c * step : 2 * (c + 1) * step], w_ref[both, :], TN, preferred_element_type=F32)
    part[...] = partial.astype(BF16).reshape(NREP, own, width)

    pl.semaphore_wait(barrier, len(peers))

    for k in range(1, NREP):
        r = (rep + k) % NREP
        send("all", part.at[r], rsbuf.at[rep], (rs_s, k), rs_r.at[rep], (blk, r))

    z_r, z_l = (z + 1) % NZ, (z + NZ - 1) % NZ

    def a_step(s):
        right, left = z_at(-s), z_at(s)
        if s > 0:
            arrived(aall.at[right], a_r.at[right])
            arrived(aall.at[left], a_r.at[left])
        if s < NZ // 2 - 1:
            send("all", aall.at[right], aall.at[right], (ar_s, s), a_r.at[right], dev(x, z_r, yh, rep))
            send("all", aall.at[left], aall.at[left], (al_s, s), a_r.at[left], dev(x, z_l, yh, rep))
        else:
            send("all", aall.at[right, 0], aall.at[right, 0], (ar_s, s), a_r.at[right], dev(x, z_r, yh, rep))
            send("all", aall.at[left, 1], aall.at[left, 1], (al_s, s), a2_r, dev(x, z_l, yh, rep))

    def finish():
        all_left("all")

        @pl.when(is_img)
        def _():
            all_left("img")

        @pl.when(jnp.logical_not(is_img))
        def _():
            all_left("txt")

    a_step(0)

    part_rows = (slab + 16) // 2
    row = lax.broadcasted_iota(jnp.int32, (part_rows, width), 0) + core * part_rows
    col = lax.broadcasted_iota(jnp.int32, (part_rows, width), 1)
    per_x = NY * d18
    wrap = jnp.zeros_like(row)
    for k in range(1, NX):
        wrap += (row >= k * per_x).astype(jnp.int32)
    source = row + wrap * (per_x * NZ - per_x)
    for zz in range(NZ):
        perm_ref[pl.ds(zz * part_rows, part_rows), :] = jnp.where(source + per_x * zz == col, 1.0, 0.0).astype(BF16)

    ids_copy.wait()
    skip_copy.wait()
    ids = ids_ref[...]
    feature = lax.broadcasted_iota(jnp.int32, (128, rows), 0)
    wanted = jnp.where(feature < 64, ids >> 6, (ids & 63) + 64)
    hot = jnp.where(feature == wanted, 1.0, 0.0).astype(F32)
    hotb[...] = hot.T.astype(BF16).reshape(NREP, own, 128)

    for k in range(1, NREP):
        r = (rep + k) % NREP
        arrived(rsbuf.at[r], rs_r.at[r])
    my_rows = pl.ds(pl.multiple_of(rep * own, own), own)
    branch = part[rep].astype(F32)
    for k in range(1, NREP):
        branch += rsbuf[(rep + k) % NREP].astype(F32)
    pre = skip_ref[my_rows, :].astype(F32) + branch
    row_norm = jnp.sqrt(jnp.sum(pre * pre, axis=1, keepdims=True) + EPS)
    unit = pre / row_norm
    unit_ref[...] = unit
    def image_at(yy, p, cc):
        return COL * cc + NYC * p + yy

    mine_i = image_at(y, par, core)
    norm_ref[...] = jnp.broadcast_to(row_norm, (own, 128))
    emb[mine_i, :, :, pl.ds(0, width)] = unit.astype(BF16).reshape(2, own // 2, width)
    emb[mine_i, :, :, pl.ds(width, 128)] = hotb[rep].reshape(2, own // 2, 128)

    warm = warm_ref[0]
    shift = shift_ref[0]
    loss_rows = (own, 128)

    @pl.when(jnp.logical_not(is_img))
    def _():
        for h in range(2):
            for xx in (1, 0, 2):
                send("txt", emb.at[mine_i, h], txt.at[0, h], (tx_s, 2 * xx + h), tt_r.at[0, h], dev(xx, z, yh, rep))
        a_step(1)

    @pl.when(is_img)
    def _():
        def to_core(slot, k):
            send("img", emb.at[slot], emb.at[slot], (ic_s, k), im_r.at[slot], at_y(x, z, y, other))

        send("img", emb.at[mine_i], emb.at[mine_i], (im_s, 0), im_r.at[mine_i], dev(x, z_pair, yh, rep))
        for k in (2, 1, 3):
            send("img", emb.at[mine_i], emb.at[mine_i], (im_s, k), im_r.at[mine_i], at_y(x, z, (y + k) % NYC, core))
        to_core(mine_i, 0)
        pair_i = image_at(y, 1 - par, core)
        arrived(emb.at[pair_i], im_r.at[pair_i])
        for k in (2, 1, 3):
            send("img", emb.at[pair_i], emb.at[pair_i], (im_s, 3 + k), im_r.at[pair_i], at_y(x, z, (y + k) % NYC, core))
        to_core(pair_i, 1)
        for h in range(2):
            arrived(txt.at[0, h], tt_r.at[0, h])
            for k in (3, 2, 1):
                zz = z_at(2 * sign if k == 2 else -k * sign)
                send("img", txt.at[0, h], txt.at[k, h], (tt_s, 4 * h + k), tt_r.at[k, h], dev(x, zz, yh, rep))
        a_step(1)
        for i, p in enumerate((par, 1 - par)):
            for k in (1, 3, 2):
                slot = image_at((y + k) % NYC, p, core)
                arrived(emb.at[slot], im_r.at[slot])
                to_core(slot, 2 + 3 * i + k - 1)
        for k in range(COL):
            slot = COL * other + k
            arrived(emb.at[slot], im_r.at[slot])
        for h in range(2):
            for k in range(1, NZ // 2):
                arrived(txt.at[k, h], tt_r.at[k, h])

        n_i, n_t = 2 * COL * own, NZ // 2 * own
        e_i = emb[...].reshape(n_i, width + 128)
        e_t = txt[...].reshape(n_t, width + 128)
        cosine = lax.dot_general(e_i[:, :width], e_t[:, :width], NT, preferred_element_type=F32)
        same = lax.dot_general(e_i[:, width:], e_t[:, width:], NT, preferred_element_type=F32)
        target = jnp.where(same > 1.5, 1.0, -1.0).astype(F32)
        margin = -target * (warm * cosine + shift)
        decay = jnp.exp(-jnp.abs(margin))
        sigmoid = jnp.where(margin >= 0.0, 1.0, decay) / (1.0 + decay)
        coef = (-target * sigmoid * (OBJECTIVE_SCALE * warm)).astype(BF16)
        grad_i = lax.dot_general(coef, e_t[:, :width], (((1,), (0,)), ((), ())), preferred_element_type=F32)
        gi[...] = grad_i.astype(BF16).reshape(2, 2, NYC, own, width)
        for i, p in enumerate((1 - par, par)):
            send("img", gi.at[other, p], gid.at[i], (gd_s, i), gd_r.at[i], at_y(x, z, y, other))
        grad_t = lax.dot_general(coef, e_i[:, :width], TN, preferred_element_type=F32)
        gtx[...] = grad_t.astype(BF16).reshape(NZ // 2, 2, own // 2, width)
        for h in range(2):
            for k in (3, 2, 1):
                send("img", gtx.at[k, h], gtr.at[k, h], (gt_s, 4 * h + k), gt_r.at[k, h], dev(x, z_at(-k * sign), yh, rep))
        softplus = jnp.maximum(margin, 0.0) + jnp.log1p(decay)
        loss_tile = jnp.sum(softplus, axis=0, keepdims=True)
        loss_tile = jnp.sum(loss_tile, axis=1, keepdims=True)
        lbuf[0] = jnp.broadcast_to(loss_tile, (8, 128))
        send("img", lbuf.at[0], lbuf.at[1], (l_s, None), l_r, at_y(x, z, y, other))
        arrived(gid.at[0], gd_r.at[0])
        gaway[...] = (gi[core, 1 - par].astype(F32) + gid[0].astype(F32)).astype(BF16)
        for k in (2, 1, 3):
            yy = (y + k) % NYC
            send("img", gaway.at[yy], garr.at[y], (go_s, k), go_r.at[y], at_y(x, z, yy, core))
        arrived(lbuf.at[1], l_r)
        l_hi, l_lo = split_hi_lo((lbuf[0] + lbuf[1])[:1, :])
        place = lax.broadcasted_iota(jnp.int32, (own, 128), 0)
        code = jnp.where(place == 0, l_hi.astype(F32), jnp.where(place == 1, l_lo.astype(F32), 0.0)).astype(BF16)
        arrived(gid.at[1], gd_r.at[1])
        gsum[:, :, pl.ds(0, width)] = (gi[core, par].astype(F32) + gid[1].astype(F32)).astype(BF16)
        for yy in range(NYC):
            gsum[yy, :, pl.ds(width, 128)] = code
        for k in (2, 1, 3):
            yy = (y + k) % NYC
            send("img", gsum.at[yy], gir.at[y], (gi_s, k), gi_r.at[y], at_y(x, z, yy, core))
        a_step(2)
        away = gaway[y].astype(F32)
        for k in range(1, NYC):
            yy = (y + k) % NYC
            arrived(garr.at[yy], go_r.at[yy])
            away += garr[yy].astype(F32)
        gix_s[...] = away.astype(BF16)
        send("img", gix_s, gix_r, (gx_s, None), gx_r, dev(x, z_pair, yh, rep))
        for h in range(2):
            total = gtx[0, h].astype(F32)
            for k in range(1, NZ // 2):
                arrived(gtr.at[k, h], gt_r.at[k, h])
                total += gtr[k, h].astype(F32)
            tsum[h] = total.astype(BF16)
            send("img", tsum.at[h], tfin.at[x, h], (tf_s, h), tf_r.at[x, h], dev(NX - 1, z, yh, rep))
        kept = gsum[y].astype(F32)
        for k in range(1, NYC):
            yy = (y + k) % NYC
            arrived(gir.at[yy], gi_r.at[yy])
            kept += gir[yy].astype(F32)
        arrived(gix_r, gx_r)
        eacc[:, pl.ds(0, width)] = kept[:, :width] + gix_r[...].astype(F32)
        eacc[:, pl.ds(width, 128)] = kept[:, width:]

    @pl.when(jnp.logical_not(is_img))
    def _():
        a_step(2)
        total = jnp.zeros((own, width), F32)
        for xx in range(NX - 1):
            for h in range(2):
                arrived(tfin.at[xx, h], tf_r.at[xx, h])
            total += tfin[xx].reshape(own, width).astype(F32)
        eacc[:, pl.ds(0, width)] = total
        eacc[:, pl.ds(width, 128)] = jnp.zeros((own, 128), F32)

    emb_grad = eacc[:, pl.ds(0, width)]
    col_loss = jnp.sum(eacc[:, pl.ds(width, 128)], axis=0, keepdims=True)
    unit = unit_ref[...]
    along = jnp.sum(unit * emb_grad, axis=1, keepdims=True)
    pre_grad = ((emb_grad - unit * along) / norm_ref[:, :1]).astype(BF16)
    gall[rep] = pre_grad
    for k in range(1, NREP):
        r = (rep + k) % NREP
        send("all", gall.at[rep], gall.at[rep], (ga_s, k), ga_r.at[rep], (blk, r))
    a_step(3)
    for k in range(1, NREP):
        r = (rep + k) % NREP
        arrived(gall.at[r], ga_r.at[r])

    g_block = gall[...].reshape(rows, width)
    g_t = lax.dot_general(perm_ref[...], g_block, NT, preferred_element_type=F32)
    gts[...] = g_t.astype(BF16).reshape(NZ, part_rows, rows)
    l_hi, l_lo = split_hi_lo(col_loss)
    place = lax.broadcasted_iota(jnp.int32, (16, 128), 0)
    code = jnp.where(place == 0, l_hi.astype(F32), jnp.where(place == 1, l_lo.astype(F32), 0.0)).astype(BF16)

    @pl.when(core == 1)
    def _():
        for zz in range(NZ):
            gts[zz, pl.ds(part_rows - 16, 16), :] = code

    for i, k in enumerate((4, 3, 5, 2, 6, 1, 7)):
        send("all", gts.at[z_at(k)], gtz.at[z, core], (gz_s, i), gz_r.at[z], dev(x, z_at(k), yh, rep))
    gtz[z, core] = gts[z]
    send("all", gtz.at[z, core], gtz.at[z, core], (gf_s, 0), gf_r.at[z], at_y(x, z, y, other))

    aint[...] = lax.dot_general(w_ref[...], g_block, NT, preferred_element_type=F32)
    for t in range(2):

        @pl.when(is_img if t == 0 else jnp.logical_not(is_img))
        def _():
            hid_ref[...] = aint[pl.ds(t, ffq, stride=2), :].astype(BF16)

    far = z_at(NZ // 2)
    arrived(aall.at[far, 0], a_r.at[far])
    arrived(aall.at[far, 1], a2_r)
    for i, k in enumerate((1, 7, 2, 6, 3, 5, 4)):
        zz = z_at(k)
        arrived(gtz.at[zz, core], gz_r.at[zz])
        send("all", gtz.at[zz, core], gtz.at[zz, core], (gf_s, i + 1), gf_r.at[zz], at_y(x, z, y, other))
    for k in range(NZ):
        arrived(gtz.at[z_at(k), other], gf_r.at[z_at(k)])

    rest = slab - part_rows
    g_cat = jnp.concatenate(
        [jnp.concatenate([gtz[zz, 0], gtz[zz, 1, :rest, :]], axis=0) for zz in range(NZ)], axis=1
    )
    a_cat = jnp.concatenate([aall[zz].reshape(2 * a_half, rows) for zz in range(NZ)], axis=1)
    lanes = pacc.shape[1]
    pacc[:, pl.ds(lanes - 128, 128)] = jnp.zeros((slab, 128), F32)
    pacc[:, pl.ds(0, a_cat.shape[0])] = lax.dot_general(g_cat, a_cat, NT, preferred_element_type=F32)
    plane = gtz[0, 1, pl.ds(rest, 16), :].astype(F32)
    for zz in range(1, NZ):
        plane += gtz[zz, 1, pl.ds(rest, 16), :].astype(F32)
    l_hi, l_lo = split_hi_lo(jnp.sum(plane, axis=0, keepdims=True))
    extra = jnp.where(place == 1, l_hi.astype(F32), jnp.where(place == 2, l_lo.astype(F32), 0.0))
    n_out = NX * NY
    full = lanes // 128 - 1
    for k in range(n_out):
        remf[k, :, pl.ds(128, 128)] = extra
        for i in range(d18 - 16):
            row = k * d18 + 16 + i
            for c in range(full):
                remf[k, pl.ds(8 * i + c, 1), pl.ds(0, 128)] = pacc[pl.ds(row, 1), pl.ds(c * 128, 128)]
            remf[k, pl.ds(8 * i, 1), pl.ds(128, 128)] = pacc[pl.ds(row, 1), pl.ds(full * 128, 128)]
        pieces[k, :, pl.ds(0, lanes)] = pacc[pl.ds(k * d18, 16), :].astype(BF16)
        pieces[k, :, pl.ds(lanes, 256)] = remf[k].astype(BF16)
    mine = x * NY + yh
    for i, (dx, dy) in enumerate(((2, 1), (1, 1), (3, 1), (2, 0), (0, 1), (1, 0), (3, 0))):
        xx, yy = (x + dx) % NX, (yh + dy) % NY
        send("all", pieces.at[xx * NY + yy], fin.at[mine], (pc_s, i), pc_r.at[mine], dev(xx, z, yy, rep))
    fin[mine] = pieces[mine]
    for j in range(1, n_out):
        k = (mine + j) % n_out
        arrived(fin.at[k], pc_r.at[k])
    n_img_out = (NX - 1) * NY
    tower = [fin[0].astype(F32), fin[n_img_out].astype(F32)]
    for k in range(1, n_img_out):
        tower[0] += fin[k].astype(F32)
    for k in range(n_img_out + 1, n_out):
        tower[1] += fin[k].astype(F32)
    for t in range(2):
        for d in range(16):
            wg_ref[d, pl.ds(t, 1), :] = tower[t][d : d + 1, :ffq]
        for i in range(d18 - 16):
            for c in range(full):
                wg_ref[16 + i, pl.ds(t, 1), pl.ds(c * 128, 128)] = tower[t][8 * i + c : 8 * i + c + 1, lanes : lanes + 128]
            last = ffq - full * 128
            wg_ref[16 + i, pl.ds(t, 1), pl.ds(full * 128, last)] = tower[t][8 * i : 8 * i + 1, lanes + 128 : lanes + 128 + last]
    both = tower[0][1, lanes + 128] + tower[0][2, lanes + 128]
    loss_ref[0] = both / (NY * n_img)

    finish()


def local(
    activated_neurons,
    skip_stream_input,
    downward_projection_weights,
    description_cluster_id,
    score_warmth_param,
    score_shift_term,
):
    rows, ffq = activated_neurons.shape
    width = skip_stream_input.shape[1]
    n_blk = lax.axis_size("blk")
    d18 = width // n_blk
    own = rows // NREP
    slab = width // NZ
    ffp = -(-ffq // 32) * 32
    n_img = rows * n_blk * 3 // 4
    lanes = -(-ffq // 128) * 128
    vmem = pl.BlockSpec(memory_space=pltpu.VMEM)
    hbm = pl.BlockSpec(memory_space=pl.ANY)
    smem = pl.BlockSpec(memory_space=pltpu.SMEM)
    dma = pltpu.SemaphoreType.DMA
    hid_t, wg_t, loss = pl.pallas_call(
        functools.partial(kernel, rows, width, ffq, n_img),
        out_shape=(
            jax.ShapeDtypeStruct((ffq, rows), BF16),
            jax.ShapeDtypeStruct((d18, 2, ffq), F32),
            jax.ShapeDtypeStruct((1,), F32),
        ),
        in_specs=[hbm, hbm, hbm, smem, smem, hbm],
        out_specs=(vmem, vmem, smem),
        scratch_shapes=[
            pltpu.VMEM((ffq, rows), BF16),
            pltpu.VMEM((rows, width), BF16),
            pltpu.VMEM((1, rows), jnp.int32),
            pltpu.VMEM((ffq, 2, width), BF16),
            pltpu.VMEM((2 * ffq, width), BF16),
            pltpu.VMEM((2 * ffq, rows), F32),
            pltpu.VMEM((NZ * (slab + 16) // 2, width), BF16),
            pltpu.VMEM((NZ, 2, ffp // 2, rows), BF16),
            pltpu.VMEM((NREP, own, width), BF16),
            pltpu.VMEM((NREP, own, width), BF16),
            pltpu.VMEM((2 * COL, 2, own // 2, width + 128), BF16),
            pltpu.VMEM((NZ // 2, 2, own // 2, width + 128), BF16),
            pltpu.VMEM((2, 8, 128), F32),
            pltpu.VMEM((2, 2, NYC, own, width), BF16),
            pltpu.VMEM((2, NYC, own, width), BF16),
            pltpu.VMEM((NYC, own, width), BF16),
            pltpu.VMEM((NYC, own, width), BF16),
            pltpu.VMEM((NYC, own, width + 128), BF16),
            pltpu.VMEM((NYC, own, width + 128), BF16),
            pltpu.VMEM((own, width), BF16),
            pltpu.VMEM((own, width), BF16),
            pltpu.VMEM((NZ // 2, 2, own // 2, width), BF16),
            pltpu.VMEM((NZ // 2, 2, own // 2, width), BF16),
            pltpu.VMEM((2, own // 2, width), BF16),
            pltpu.VMEM((NX - 1, 2, own // 2, width), BF16),
            pltpu.VMEM((NREP, own, 128), BF16),
            pltpu.VMEM((NREP, own, width), BF16),
            pltpu.VMEM((own, width + 128), F32),
            pltpu.VMEM((NZ, (slab + 16) // 2, rows), BF16),
            pltpu.VMEM((NZ, 2, (slab + 16) // 2, rows), BF16),
            pltpu.VMEM((slab, lanes), F32),
            pltpu.VMEM((NX * NY, 16, 256), F32),
            pltpu.VMEM((NX * NY, 16, lanes + 256), BF16),
            pltpu.VMEM((NX * NY, 16, lanes + 256), BF16),
            pltpu.VMEM((own, width), F32),
            pltpu.VMEM((own, 128), F32),
            dma((4,)),
            dma((3,)),
            dma((NREP,)),
            dma((NREP,)),
            dma((7,)),
            dma((COL,)),
            dma((2 * COL,)),
            dma((2 * (NX - 1),)),
            dma((NZ,)),
            dma((NZ // 2, 2)),
            dma,
            dma,
            dma((NYC,)),
            dma((NYC,)),
            dma((NYC,)),
            dma((NYC,)),
            dma,
            dma,
            dma((2,)),
            dma((2,)),
            dma((NZ,)),
            dma((NZ // 2, 2)),
            dma((2,)),
            dma((NX - 1, 2)),
            dma((NREP,)),
            dma((NREP,)),
            dma((NZ,)),
            dma((NZ,)),
            dma((NZ,)),
            dma((NZ,)),
            dma((NX * NY,)),
            dma((NX * NY,)),
            dma((NZ // 2,)),
            dma((NZ // 2,)),
            dma((NZ,)),
            dma,
        ],
        compiler_params=pltpu.CompilerParams(
            collective_id=0, has_side_effects=True, vmem_limit_bytes=53 * 1024 * 1024 + 512 * 1024
        ),
        cost_estimate=pl.CostEstimate(flops=2 * 10**9, bytes_accessed=10**7, transcendentals=10**6),
    )(
        activated_neurons.T,
        skip_stream_input,
        description_cluster_id.reshape(1, rows),
        score_warmth_param,
        score_shift_term,
        jnp.transpose(downward_projection_weights, (1, 0, 2)),
    )
    return hid_t.T, jnp.transpose(wg_t, (1, 2, 0)), loss


def solution(mesh):
    placed = (P("blk", "rep"), P("blk", None), P(None, "rep", None), P("blk"), P(), P())
    return jax.shard_map(
        local,
        mesh=mesh,
        in_specs=placed,
        out_specs=(P("blk", "rep"), P(None, "rep", "blk"), P()),
        check_vma=False,
    )
```

```python
import functools

import jax
import jax.numpy as jnp
from jax import lax
from jax.experimental import pallas as pl
from jax.experimental.pallas import tpu as pltpu
from jax.sharding import PartitionSpec as P

EPS = 1e-06
OBJECTIVE_SCALE = 16.0
F32 = jnp.float32
BF16 = jnp.bfloat16
MESH = pl.DeviceIdType.MESH
NT = (((1,), (1,)), ((), ()))
TN = (((0,), (0,)), ((), ()))

NX, NZ, NY, NREP = 4, 8, 2, 4
COL = NY * NREP
NYC = 4


def split_hi_lo(v):
    hi = v.astype(BF16)
    return hi, (v - hi.astype(F32)).astype(BF16)


def kernel(
    rows,
    width,
    ffq,
    n_img,
    at_hbm,
    skip_hbm,
    ids_hbm,
    warm_ref,
    shift_ref,
    w_hbm,
    hid_ref,
    wg_ref,
    loss_ref,
    at_ref,
    skip_ref,
    ids_ref,
    wnat,
    w_ref,
    aint,
    perm_ref,
    aall,
    part,
    rsbuf,
    emb,
    txt,
    lbuf,
    gi,
    gid,
    gaway,
    garr,
    gsum,
    gir,
    gix_s,
    gix_r,
    gtx,
    gtr,
    tsum,
    tfin,
    hotb,
    gall,
    eacc,
    gts,
    gtz,
    pacc,
    remf,
    pieces,
    fin,
    unit_ref,
    norm_ref,
    w_sem,
    in_sem,
    rs_s,
    rs_r,
    im_s,
    ic_s,
    im_r,
    tx_s,
    tt_s,
    tt_r,
    l_s,
    l_r,
    go_s,
    go_r,
    gi_s,
    gi_r,
    gx_s,
    gx_r,
    gd_s,
    gd_r,
    gt_s,
    gt_r,
    tf_s,
    tf_r,
    ga_s,
    ga_r,
    gz_s,
    gz_r,
    gf_s,
    gf_r,
    pc_s,
    pc_r,
    ar_s,
    al_s,
    a_r,
    a2_r,
):
    own = rows // NREP
    d18 = width // (NX * NZ * NY)
    slab = width // NZ
    blk = lax.axis_index("blk")
    rep = lax.axis_index("rep")
    x = blk // (NZ * NY)
    z = (blk // NY) % NZ
    yh = blk % NY
    y = yh * 2 + rep // 2
    core = rep % 2
    other = 1 - core
    par = z % 2
    sign = 1 - 2 * par
    z_pair = z + 1 - 2 * par
    is_img = x < NX - 1

    def dev(xx, zz, yy, rr):
        return ((xx * NZ + zz) * NY + yy, rr)

    def z_at(offset):
        return (z + NZ + offset) % NZ

    def at_y(xx, zz, yy, cc):
        return dev(xx, zz, yy // 2, (yy % 2) * 2 + cc)

    def rcopy(src, dst, ssem, rsem, device):
        return pltpu.make_async_remote_copy(
            src_ref=src, dst_ref=dst, send_sem=ssem, recv_sem=rsem, device_id=device, device_id_type=MESH
        )

    here = (blk, rep)

    def arrived(ref, rsem):
        rcopy(ref, ref, rsem, rsem, here).wait_recv()

    sent = {"all": [], "img": [], "txt": []}

    def send(group, src, dst, ssem, rsem, device):
        sem, k = ssem
        rcopy(src, dst, sem if k is None else sem.at[k], rsem, device).start()
        base = src.ref if hasattr(src, "ref") else src
        entry = (base, len(base.shape) - len(src.shape), sem, k)
        if all(e[2] is not sem or e[3] != k for e in sent[group]):
            sent[group].append(entry)

    def all_left(group):
        for ref, block, sem, k in sent[group]:
            ref = ref.at[(0,) * block] if block else ref
            sem = sem if k is None else sem.at[k]
            rcopy(ref, ref, sem, sem, here).wait_send()

    barrier = pltpu.get_barrier_semaphore()
    peers = [at_y(x, z, (y + k) % NYC, core) for k in range(1, NYC)]
    peers += [dev(x, z, yh, (rep // 2) * 2 + other), dev(x, z, yh, (1 - rep // 2) * 2 + other)]
    peers += [dev(x, (z + k) % NZ, yh, rep) for k in range(1, NZ)]
    peers += [dev((x + k) % NX, z, yy, rep) for k in range(1, NX) for yy in range(NY)]
    for peer in peers:
        pl.semaphore_signal(barrier, inc=1, device_id=peer, device_id_type=MESH)

    a_copy = pltpu.make_async_copy(at_hbm, at_ref, in_sem.at[0])
    a_copy.start()
    n_cut = 2
    step = ffq // n_cut
    cuts = [pl.ds(c * step, step) for c in range(n_cut)]
    w_copies = [pltpu.make_async_copy(w_hbm.at[cut], wnat.at[cut], w_sem.at[c]) for c, cut in enumerate(cuts)]
    for copy in w_copies:
        copy.start()
    skip_copy = pltpu.make_async_copy(skip_hbm, skip_ref, in_sem.at[1])
    ids_copy = pltpu.make_async_copy(ids_hbm, ids_ref, in_sem.at[2])
    skip_copy.start()
    ids_copy.start()

    aint[...] = jnp.zeros_like(aint)
    a_copy.wait()
    for t in range(2):

        @pl.when(is_img if t == 0 else jnp.logical_not(is_img))
        def _():
            aint[pl.ds(t, ffq, stride=2), :] = at_ref[...].astype(F32)

    a_int = aint[...].astype(BF16)
    a_half = aall.shape[2]
    aall[z, 1, pl.ds(a_half - 16, 16), :] = jnp.zeros((16, rows), BF16)
    aall[z, 0] = at_ref[pl.ds(0, a_half), :]
    aall[z, 1, pl.ds(0, ffq - a_half), :] = at_ref[pl.ds(a_half, ffq - a_half), :]
    partial = jnp.zeros((rows, width), F32)
    for c, copy in enumerate(w_copies):
        copy.wait()
        both = pl.ds(2 * c * step, 2 * step)
        w_ref[both, :] = wnat[cuts[c]].reshape(2 * step, width)
        partial += lax.dot_general(a_int[2 * c * step : 2 * (c + 1) * step], w_ref[both, :], TN, preferred_element_type=F32)
    part[...] = partial.astype(BF16).reshape(NREP, own, width)

    pl.semaphore_wait(barrier, len(peers))

    for k in range(1, NREP):
        r = (rep + k) % NREP
        send("all", part.at[r], rsbuf.at[rep], (rs_s, k), rs_r.at[rep], (blk, r))

    z_r, z_l = (z + 1) % NZ, (z + NZ - 1) % NZ

    def a_step(s):
        right, left = z_at(-s), z_at(s)
        if s > 0:
            arrived(aall.at[right], a_r.at[right])
            arrived(aall.at[left], a_r.at[left])
        if s < NZ // 2 - 1:
            send("all", aall.at[right], aall.at[right], (ar_s, s), a_r.at[right], dev(x, z_r, yh, rep))
            send("all", aall.at[left], aall.at[left], (al_s, s), a_r.at[left], dev(x, z_l, yh, rep))
        else:
            send("all", aall.at[right, 0], aall.at[right, 0], (ar_s, s), a_r.at[right], dev(x, z_r, yh, rep))
            send("all", aall.at[left, 1], aall.at[left, 1], (al_s, s), a2_r, dev(x, z_l, yh, rep))

    def finish():
        all_left("all")

        @pl.when(is_img)
        def _():
            all_left("img")

        @pl.when(jnp.logical_not(is_img))
        def _():
            all_left("txt")

    a_step(0)

    part_rows = (slab + 16) // 2
    row = lax.broadcasted_iota(jnp.int32, (part_rows, width), 0) + core * part_rows
    col = lax.broadcasted_iota(jnp.int32, (part_rows, width), 1)
    per_x = NY * d18
    wrap = jnp.zeros_like(row)
    for k in range(1, NX):
        wrap += (row >= k * per_x).astype(jnp.int32)
    source = row + wrap * (per_x * NZ - per_x)
    for zz in range(NZ):
        perm_ref[pl.ds(zz * part_rows, part_rows), :] = jnp.where(source + per_x * zz == col, 1.0, 0.0).astype(BF16)

    ids_copy.wait()
    skip_copy.wait()
    ids = ids_ref[...]
    feature = lax.broadcasted_iota(jnp.int32, (128, rows), 0)
    wanted = jnp.where(feature < 64, ids >> 6, (ids & 63) + 64)
    hot = jnp.where(feature == wanted, 1.0, 0.0).astype(F32)
    hotb[...] = hot.T.astype(BF16).reshape(NREP, own, 128)

    for k in range(1, NREP):
        r = (rep + k) % NREP
        arrived(rsbuf.at[r], rs_r.at[r])
    my_rows = pl.ds(pl.multiple_of(rep * own, own), own)
    branch = part[rep].astype(F32)
    for k in range(1, NREP):
        branch += rsbuf[(rep + k) % NREP].astype(F32)
    pre = skip_ref[my_rows, :].astype(F32) + branch
    row_norm = jnp.sqrt(jnp.sum(pre * pre, axis=1, keepdims=True) + EPS)
    unit = pre / row_norm
    unit_ref[...] = unit
    def image_at(yy, p, cc):
        return COL * cc + NYC * p + yy

    mine_i = image_at(y, par, core)
    norm_ref[...] = jnp.broadcast_to(row_norm, (own, 128))
    emb[mine_i, :, :, pl.ds(0, width)] = unit.astype(BF16).reshape(2, own // 2, width)
    emb[mine_i, :, :, pl.ds(width, 128)] = hotb[rep].reshape(2, own // 2, 128)

    warm = warm_ref[0]
    shift = shift_ref[0]
    loss_rows = (own, 128)

    @pl.when(jnp.logical_not(is_img))
    def _():
        for h in range(2):
            for xx in (1, 0, 2):
                send("txt", emb.at[mine_i, h], txt.at[0, h], (tx_s, 2 * xx + h), tt_r.at[0, h], dev(xx, z, yh, rep))
        a_step(1)

    @pl.when(is_img)
    def _():
        def to_core(slot, k):
            send("img", emb.at[slot], emb.at[slot], (ic_s, k), im_r.at[slot], at_y(x, z, y, other))

        send("img", emb.at[mine_i], emb.at[mine_i], (im_s, 0), im_r.at[mine_i], dev(x, z_pair, yh, rep))
        for k in (2, 1, 3):
            send("img", emb.at[mine_i], emb.at[mine_i], (im_s, k), im_r.at[mine_i], at_y(x, z, (y + k) % NYC, core))
        to_core(mine_i, 0)
        pair_i = image_at(y, 1 - par, core)
        arrived(emb.at[pair_i], im_r.at[pair_i])
        for k in (2, 1, 3):
            send("img", emb.at[pair_i], emb.at[pair_i], (im_s, 3 + k), im_r.at[pair_i], at_y(x, z, (y + k) % NYC, core))
        to_core(pair_i, 1)
        for h in range(2):
            arrived(txt.at[0, h], tt_r.at[0, h])
            for k in (3, 2, 1):
                zz = z_at(2 * sign if k == 2 else -k * sign)
                send("img", txt.at[0, h], txt.at[k, h], (tt_s, 4 * h + k), tt_r.at[k, h], dev(x, zz, yh, rep))
        a_step(1)
        for i, p in enumerate((par, 1 - par)):
            for k in (1, 3, 2):
                slot = image_at((y + k) % NYC, p, core)
                arrived(emb.at[slot], im_r.at[slot])
                to_core(slot, 2 + 3 * i + k - 1)
        for k in range(COL):
            slot = COL * other + k
            arrived(emb.at[slot], im_r.at[slot])
        for h in range(2):
            for k in range(1, NZ // 2):
                arrived(txt.at[k, h], tt_r.at[k, h])

        n_i, n_t = 2 * COL * own, NZ // 2 * own
        e_i = emb[...].reshape(n_i, width + 128)
        e_t = txt[...].reshape(n_t, width + 128)
        cosine = lax.dot_general(e_i[:, :width], e_t[:, :width], NT, preferred_element_type=F32)
        same = lax.dot_general(e_i[:, width:], e_t[:, width:], NT, preferred_element_type=F32)
        target = jnp.where(same > 1.5, 1.0, -1.0).astype(F32)
        margin = -target * (warm * cosine + shift)
        decay = jnp.exp(-jnp.abs(margin))
        sigmoid = jnp.where(margin >= 0.0, 1.0, decay) / (1.0 + decay)
        coef = (-target * sigmoid * (OBJECTIVE_SCALE * warm)).astype(BF16)
        grad_i = lax.dot_general(coef, e_t[:, :width], (((1,), (0,)), ((), ())), preferred_element_type=F32)
        gi[...] = grad_i.astype(BF16).reshape(2, 2, NYC, own, width)
        for i, p in enumerate((1 - par, par)):
            send("img", gi.at[other, p], gid.at[i], (gd_s, i), gd_r.at[i], at_y(x, z, y, other))
        grad_t = lax.dot_general(coef, e_i[:, :width], TN, preferred_element_type=F32)
        gtx[...] = grad_t.astype(BF16).reshape(NZ // 2, 2, own // 2, width)
        for h in range(2):
            for k in (3, 2, 1):
                send("img", gtx.at[k, h], gtr.at[k, h], (gt_s, 4 * h + k), gt_r.at[k, h], dev(x, z_at(-k * sign), yh, rep))
        softplus = jnp.maximum(margin, 0.0) + jnp.log1p(decay)
        loss_tile = jnp.sum(softplus, axis=0, keepdims=True)
        loss_tile = jnp.sum(loss_tile, axis=1, keepdims=True)
        lbuf[0] = jnp.broadcast_to(loss_tile, (8, 128))
        send("img", lbuf.at[0], lbuf.at[1], (l_s, None), l_r, at_y(x, z, y, other))
        arrived(gid.at[0], gd_r.at[0])
        gaway[...] = (gi[core, 1 - par].astype(F32) + gid[0].astype(F32)).astype(BF16)
        for k in (2, 1, 3):
            yy = (y + k) % NYC
            send("img", gaway.at[yy], garr.at[y], (go_s, k), go_r.at[y], at_y(x, z, yy, core))
        arrived(lbuf.at[1], l_r)
        l_hi, l_lo = split_hi_lo((lbuf[0] + lbuf[1])[:1, :])
        place = lax.broadcasted_iota(jnp.int32, (own, 128), 0)
        code = jnp.where(place == 0, l_hi.astype(F32), jnp.where(place == 1, l_lo.astype(F32), 0.0)).astype(BF16)
        arrived(gid.at[1], gd_r.at[1])
        gsum[:, :, pl.ds(0, width)] = (gi[core, par].astype(F32) + gid[1].astype(F32)).astype(BF16)
        for yy in range(NYC):
            gsum[yy, :, pl.ds(width, 128)] = code
        for k in (2, 1, 3):
            yy = (y + k) % NYC
            send("img", gsum.at[yy], gir.at[y], (gi_s, k), gi_r.at[y], at_y(x, z, yy, core))
        a_step(2)
        away = gaway[y].astype(F32)
        for k in range(1, NYC):
            yy = (y + k) % NYC
            arrived(garr.at[yy], go_r.at[yy])
            away += garr[yy].astype(F32)
        gix_s[...] = away.astype(BF16)
        send("img", gix_s, gix_r, (gx_s, None), gx_r, dev(x, z_pair, yh, rep))
        for h in range(2):
            total = gtx[0, h].astype(F32)
            for k in range(1, NZ // 2):
                arrived(gtr.at[k, h], gt_r.at[k, h])
                total += gtr[k, h].astype(F32)
            tsum[h] = total.astype(BF16)
            send("img", tsum.at[h], tfin.at[x, h], (tf_s, h), tf_r.at[x, h], dev(NX - 1, z, yh, rep))
        kept = gsum[y].astype(F32)
        for k in range(1, NYC):
            yy = (y + k) % NYC
            arrived(gir.at[yy], gi_r.at[yy])
            kept += gir[yy].astype(F32)
        arrived(gix_r, gx_r)
        eacc[:, pl.ds(0, width)] = kept[:, :width] + gix_r[...].astype(F32)
        eacc[:, pl.ds(width, 128)] = kept[:, width:]

    @pl.when(jnp.logical_not(is_img))
    def _():
        a_step(2)
        total = jnp.zeros((own, width), F32)
        for xx in range(NX - 1):
            for h in range(2):
                arrived(tfin.at[xx, h], tf_r.at[xx, h])
            total += tfin[xx].reshape(own, width).astype(F32)
        eacc[:, pl.ds(0, width)] = total
        eacc[:, pl.ds(width, 128)] = jnp.zeros((own, 128), F32)

    emb_grad = eacc[:, pl.ds(0, width)]
    col_loss = jnp.sum(eacc[:, pl.ds(width, 128)], axis=0, keepdims=True)
    unit = unit_ref[...]
    along = jnp.sum(unit * emb_grad, axis=1, keepdims=True)
    pre_grad = ((emb_grad - unit * along) / norm_ref[:, :1]).astype(BF16)
    gall[rep] = pre_grad
    for k in range(1, NREP):
        r = (rep + k) % NREP
        send("all", gall.at[rep], gall.at[rep], (ga_s, k), ga_r.at[rep], (blk, r))
    a_step(3)
    for k in range(1, NREP):
        r = (rep + k) % NREP
        arrived(gall.at[r], ga_r.at[r])

    g_block = gall[...].reshape(rows, width)
    g_t = lax.dot_general(perm_ref[...], g_block, NT, preferred_element_type=F32)
    gts[...] = g_t.astype(BF16).reshape(NZ, part_rows, rows)
    l_hi, l_lo = split_hi_lo(col_loss)
    place = lax.broadcasted_iota(jnp.int32, (16, 128), 0)
    code = jnp.where(place == 0, l_hi.astype(F32), jnp.where(place == 1, l_lo.astype(F32), 0.0)).astype(BF16)

    @pl.when(core == 1)
    def _():
        for zz in range(NZ):
            gts[zz, pl.ds(part_rows - 16, 16), :] = code

    for i, k in enumerate((4, 3, 5, 2, 6, 1, 7)):
        send("all", gts.at[z_at(k)], gtz.at[z, core], (gz_s, i), gz_r.at[z], dev(x, z_at(k), yh, rep))
    gtz[z, core] = gts[z]
    send("all", gtz.at[z, core], gtz.at[z, core], (gf_s, 0), gf_r.at[z], at_y(x, z, y, other))

    far = z_at(NZ // 2)
    arrived(aall.at[far, 0], a_r.at[far])
    arrived(aall.at[far, 1], a2_r)
    for i, k in enumerate((1, 7, 2, 6, 3, 5, 4)):
        zz = z_at(k)
        arrived(gtz.at[zz, core], gz_r.at[zz])
        send("all", gtz.at[zz, core], gtz.at[zz, core], (gf_s, i + 1), gf_r.at[zz], at_y(x, z, y, other))
    for k in range(NZ):
        arrived(gtz.at[z_at(k), other], gf_r.at[z_at(k)])

    rest = slab - part_rows
    g_cat = jnp.concatenate(
        [jnp.concatenate([gtz[zz, 0], gtz[zz, 1, :rest, :]], axis=0) for zz in range(NZ)], axis=1
    )
    a_cat = jnp.concatenate([aall[zz].reshape(2 * a_half, rows) for zz in range(NZ)], axis=1)
    lanes = pacc.shape[1]
    pacc[:, pl.ds(lanes - 128, 128)] = jnp.zeros((slab, 128), F32)
    pacc[:, pl.ds(0, a_cat.shape[0])] = lax.dot_general(g_cat, a_cat, NT, preferred_element_type=F32)
    plane = gtz[0, 1, pl.ds(rest, 16), :].astype(F32)
    for zz in range(1, NZ):
        plane += gtz[zz, 1, pl.ds(rest, 16), :].astype(F32)
    l_hi, l_lo = split_hi_lo(jnp.sum(plane, axis=0, keepdims=True))
    extra = jnp.where(place == 1, l_hi.astype(F32), jnp.where(place == 2, l_lo.astype(F32), 0.0))
    n_out = NX * NY
    full = lanes // 128 - 1
    for k in range(n_out):
        remf[k, :, pl.ds(128, 128)] = extra
        for i in range(d18 - 16):
            row = k * d18 + 16 + i
            for c in range(full):
                remf[k, pl.ds(8 * i + c, 1), pl.ds(0, 128)] = pacc[pl.ds(row, 1), pl.ds(c * 128, 128)]
            remf[k, pl.ds(8 * i, 1), pl.ds(128, 128)] = pacc[pl.ds(row, 1), pl.ds(full * 128, 128)]
        pieces[k, :, pl.ds(0, lanes)] = pacc[pl.ds(k * d18, 16), :].astype(BF16)
        pieces[k, :, pl.ds(lanes, 256)] = remf[k].astype(BF16)
    mine = x * NY + yh
    for i, (dx, dy) in enumerate(((2, 1), (1, 1), (3, 1), (2, 0), (0, 1), (1, 0), (3, 0))):
        xx, yy = (x + dx) % NX, (yh + dy) % NY
        send("all", pieces.at[xx * NY + yy], fin.at[mine], (pc_s, i), pc_r.at[mine], dev(xx, z, yy, rep))
    fin[mine] = pieces[mine]
    aint[...] = lax.dot_general(w_ref[...], gall[...].reshape(rows, width), NT, preferred_element_type=F32)
    for t in range(2):

        @pl.when(is_img if t == 0 else jnp.logical_not(is_img))
        def _():
            hid_ref[...] = aint[pl.ds(t, ffq, stride=2), :].astype(BF16)

    for j in range(1, n_out):
        k = (mine + j) % n_out
        arrived(fin.at[k], pc_r.at[k])
    n_img_out = (NX - 1) * NY
    tower = [fin[0].astype(F32), fin[n_img_out].astype(F32)]
    for k in range(1, n_img_out):
        tower[0] += fin[k].astype(F32)
    for k in range(n_img_out + 1, n_out):
        tower[1] += fin[k].astype(F32)
    for t in range(2):
        for d in range(16):
            wg_ref[d, pl.ds(t, 1), :] = tower[t][d : d + 1, :ffq]
        for i in range(d18 - 16):
            for c in range(full):
                wg_ref[16 + i, pl.ds(t, 1), pl.ds(c * 128, 128)] = tower[t][8 * i + c : 8 * i + c + 1, lanes : lanes + 128]
            last = ffq - full * 128
            wg_ref[16 + i, pl.ds(t, 1), pl.ds(full * 128, last)] = tower[t][8 * i : 8 * i + 1, lanes + 128 : lanes + 128 + last]
    both = tower[0][1, lanes + 128] + tower[0][2, lanes + 128]
    loss_ref[0] = both / (NY * n_img)

    finish()


def local(
    activated_neurons,
    skip_stream_input,
    downward_projection_weights,
    description_cluster_id,
    score_warmth_param,
    score_shift_term,
):
    rows, ffq = activated_neurons.shape
    width = skip_stream_input.shape[1]
    n_blk = lax.axis_size("blk")
    d18 = width // n_blk
    own = rows // NREP
    slab = width // NZ
    ffp = -(-ffq // 32) * 32
    n_img = rows * n_blk * 3 // 4
    lanes = -(-ffq // 128) * 128
    vmem = pl.BlockSpec(memory_space=pltpu.VMEM)
    hbm = pl.BlockSpec(memory_space=pl.ANY)
    smem = pl.BlockSpec(memory_space=pltpu.SMEM)
    dma = pltpu.SemaphoreType.DMA
    hid_t, wg_t, loss = pl.pallas_call(
        functools.partial(kernel, rows, width, ffq, n_img),
        out_shape=(
            jax.ShapeDtypeStruct((ffq, rows), BF16),
            jax.ShapeDtypeStruct((d18, 2, ffq), F32),
            jax.ShapeDtypeStruct((1,), F32),
        ),
        in_specs=[hbm, hbm, hbm, smem, smem, hbm],
        out_specs=(vmem, vmem, smem),
        scratch_shapes=[
            pltpu.VMEM((ffq, rows), BF16),
            pltpu.VMEM((rows, width), BF16),
            pltpu.VMEM((1, rows), jnp.int32),
            pltpu.VMEM((ffq, 2, width), BF16),
            pltpu.VMEM((2 * ffq, width), BF16),
            pltpu.VMEM((2 * ffq, rows), F32),
            pltpu.VMEM((NZ * (slab + 16) // 2, width), BF16),
            pltpu.VMEM((NZ, 2, ffp // 2, rows), BF16),
            pltpu.VMEM((NREP, own, width), BF16),
            pltpu.VMEM((NREP, own, width), BF16),
            pltpu.VMEM((2 * COL, 2, own // 2, width + 128), BF16),
            pltpu.VMEM((NZ // 2, 2, own // 2, width + 128), BF16),
            pltpu.VMEM((2, 8, 128), F32),
            pltpu.VMEM((2, 2, NYC, own, width), BF16),
            pltpu.VMEM((2, NYC, own, width), BF16),
            pltpu.VMEM((NYC, own, width), BF16),
            pltpu.VMEM((NYC, own, width), BF16),
            pltpu.VMEM((NYC, own, width + 128), BF16),
            pltpu.VMEM((NYC, own, width + 128), BF16),
            pltpu.VMEM((own, width), BF16),
            pltpu.VMEM((own, width), BF16),
            pltpu.VMEM((NZ // 2, 2, own // 2, width), BF16),
            pltpu.VMEM((NZ // 2, 2, own // 2, width), BF16),
            pltpu.VMEM((2, own // 2, width), BF16),
            pltpu.VMEM((NX - 1, 2, own // 2, width), BF16),
            pltpu.VMEM((NREP, own, 128), BF16),
            pltpu.VMEM((NREP, own, width), BF16),
            pltpu.VMEM((own, width + 128), F32),
            pltpu.VMEM((NZ, (slab + 16) // 2, rows), BF16),
            pltpu.VMEM((NZ, 2, (slab + 16) // 2, rows), BF16),
            pltpu.VMEM((slab, lanes), F32),
            pltpu.VMEM((NX * NY, 16, 256), F32),
            pltpu.VMEM((NX * NY, 16, lanes + 256), BF16),
            pltpu.VMEM((NX * NY, 16, lanes + 256), BF16),
            pltpu.VMEM((own, width), F32),
            pltpu.VMEM((own, 128), F32),
            dma((4,)),
            dma((3,)),
            dma((NREP,)),
            dma((NREP,)),
            dma((7,)),
            dma((COL,)),
            dma((2 * COL,)),
            dma((2 * (NX - 1),)),
            dma((NZ,)),
            dma((NZ // 2, 2)),
            dma,
            dma,
            dma((NYC,)),
            dma((NYC,)),
            dma((NYC,)),
            dma((NYC,)),
            dma,
            dma,
            dma((2,)),
            dma((2,)),
            dma((NZ,)),
            dma((NZ // 2, 2)),
            dma((2,)),
            dma((NX - 1, 2)),
            dma((NREP,)),
            dma((NREP,)),
            dma((NZ,)),
            dma((NZ,)),
            dma((NZ,)),
            dma((NZ,)),
            dma((NX * NY,)),
            dma((NX * NY,)),
            dma((NZ // 2,)),
            dma((NZ // 2,)),
            dma((NZ,)),
            dma,
        ],
        compiler_params=pltpu.CompilerParams(
            collective_id=0, has_side_effects=True, vmem_limit_bytes=53 * 1024 * 1024 + 512 * 1024
        ),
        cost_estimate=pl.CostEstimate(flops=2 * 10**9, bytes_accessed=10**7, transcendentals=10**6),
    )(
        activated_neurons.T,
        skip_stream_input,
        description_cluster_id.reshape(1, rows),
        score_warmth_param,
        score_shift_term,
        jnp.transpose(downward_projection_weights, (1, 0, 2)),
    )
    return hid_t.T, jnp.transpose(wg_t, (1, 2, 0)), loss


def solution(mesh):
    placed = (P("blk", "rep"), P("blk", None), P(None, "rep", None), P("blk"), P(), P())
    return jax.shard_map(
        local,
        mesh=mesh,
        in_specs=placed,
        out_specs=(P("blk", "rep"), P(None, "rep", "blk"), P()),
        check_vma=False,
    )
```
